128 devices in a mesh: gx: 4 (over y), gy: 32 (over z, x, core).
Axes of the slice: x: 4, y: 4, z: 4, core: 2. Of those that a mesh axis runs over, the one named last changes fastest.
Arguments:
- potential_heat_value: float32 [8, 1024, 4096], P(None, ('gx', 'gy')), may hold values from -6 to 6
- saltiness_anomaly: float32 [8, 1024, 4096], P(None, ('gx', 'gy')), may hold values from -6 to 6
- zonal_current_rate: float32 [8, 1024, 4096], P(None, ('gx', 'gy')), may hold values from -0.45 to 0.45
- meridional_current_rate: float32 [8, 1024, 4096], P(None, ('gx', 'gy')), may hold values from -0.45 to 0.45
- interface_mixing_factor: float32 [7, 1024, 4096], P(None, ('gx', 'gy')), may hold values from 0.1 to 10
- free_surface_diagonal_term: float32 [1024, 4096], P(('gx', 'gy')), may hold values from 0.02 to 0.5
- surface_drive_source: float32 [1024, 4096], P(('gx', 'gy')), may hold values from -6 to 6
- ocean_patch_flags: int32 [1024], replicated, may hold values from 0 to 1, as said below
- adjacent_patch_indices: int32 [1024, 8], replicated, may hold values from -1 to 1023, as said below
Outputs:
- temperature_next: float32 [8, 1024, 4096], P(None, ('gx', 'gy'))
- salinity_next: float32 [8, 1024, 4096], P(None, ('gx', 'gy'))
- zonal_next: float32 [8, 1024, 4096], P(None, ('gx', 'gy'))
- meridional_next: float32 [8, 1024, 4096], P(None, ('gx', 'gy'))
- surface_height: float32 [1024, 4096], P(('gx', 'gy'))
The draws below stay inside these ranges and needn't reach their ends.
Inputs may be any that keep to these rules, and one draw needn't show every extreme that they name: `ocean_patch_flags`: block numbers run along the curve, 8 consecutive blocks on each device of gx+gy in order; devices 2j and 2j+1 together hold exactly 8 ocean blocks, and device 0 holds 8. `adjacent_patch_indices`: row b lists the neighbours of block b on a grid of 4 x 256 blocks, periodic east-west and closed north and south; -1 where there is none or it is land, and -1 throughout for a land block. The relation is symmetric, and a listed number differs from b by at most 7 counted around the 1024 numbers.
All inputs are finite; a program needn't handle non-finite values.
Results may differ from the reference program's by a relative error of at most 0.0001.
Values sent between devices are 32-bit elements; how exact they have to be, the bound alone decides.
A program may use at most 128 MiB of HBM per device.

```python
import math
import jax
import jax.numpy as jnp

BSIDE = 64
PATCH_POINTS = 4096
LAYER_NUMBER = 8
ITERS = 4
BLK_DEV = 8
PATCH_TOTAL = 1024
BLOCK_ROWS = 4
BLOCK_COLS = 256


def block_layout(key):
    flip_key, count_key, shuffle_key = jax.random.split(key, 3)
    device_count = PATCH_TOTAL // BLK_DEV
    pair_count = device_count // 2
    column_flip = jax.random.randint(flip_key, (BLOCK_COLS,), 0, 2)
    first_count = jax.random.randint(count_key, (pair_count,), 0, BLK_DEV + 1)
    first_count = jnp.where(jnp.arange(pair_count) == 0, BLK_DEV, first_count)
    counts = jnp.stack([first_count, BLK_DEV - first_count], axis=1).reshape(device_count)

    def shuffle_one(single_key):
        return jax.random.permutation(single_key, BLK_DEV)
    shuffled = jax.vmap(shuffle_one)(jax.random.split(shuffle_key, device_count))
    ocean = (shuffled < counts[:, None]).astype(jnp.int32).reshape(PATCH_TOTAL)
    along_curve = jnp.arange(PATCH_TOTAL)
    column = along_curve // BLOCK_ROWS
    offset = along_curve % BLOCK_ROWS
    grid_row = jnp.where(column_flip[column] == 0, offset, BLOCK_ROWS - 1 - offset)
    listed = []
    for col_step, row_step in ((1, 0), (-1, 0), (0, 1), (0, -1), (1, 1), (-1, 1), (1, -1), (-1, -1)):
        other_col = jnp.mod(column + col_step, BLOCK_COLS)
        other_row = grid_row + row_step
        inside = (other_row >= 0) & (other_row < BLOCK_ROWS)
        clipped = jnp.clip(other_row, 0, BLOCK_ROWS - 1)
        target = other_col * BLOCK_ROWS + jnp.where(column_flip[other_col] == 0, clipped, BLOCK_ROWS - 1 - clipped)
        keep = inside & (ocean[target] > 0) & (ocean > 0)
        listed.append(jnp.where(keep, target, -1))
    return (ocean, jnp.stack(listed, axis=1).astype(jnp.int32))


def draw_ocean_patch_flags(key, part):
    layout = block_layout(key)
    return layout[0]


def draw_adjacent_patch_indices(key, part):
    layout = block_layout(key)
    return layout[1]


def steps_of(key, shape, cuts, low, high):
    factor_of = 1.0
    for position, blocks in cuts:
        draws = jax.random.uniform(jax.random.fold_in(jax.random.fold_in(key, 6), position), (blocks,), jnp.float32, low / len(cuts), high / len(cuts))
        factor_of = factor_of * jnp.repeat(jnp.exp(draws), shape[position] // blocks).reshape((-1,) + (1,) * (len(shape) - 1 - position))
    return factor_of


def normal_values(stream_key, shape, spread, limit, cuts=(), dtype=jnp.bfloat16):
    result = spread * jax.random.normal(stream_key, shape, jnp.float32)
    if cuts:
        result = result * steps_of(stream_key, shape, cuts, -0.22, 0.18)
    return jnp.clip(result, -limit, limit).astype(dtype)


def setup_inputs(seed: int = 0) -> dict:
    splits = jax.random.split(jax.random.key(seed), 10)
    return {
        "potential_heat_value": normal_values(splits[0], (LAYER_NUMBER, PATCH_TOTAL, PATCH_POINTS), 1.0, 6.0, ((1, 128),), jnp.float32),
        "saltiness_anomaly": normal_values(splits[1], (LAYER_NUMBER, PATCH_TOTAL, PATCH_POINTS), 1.0, 6.0, ((1, 128),), jnp.float32),
        "zonal_current_rate": jnp.clip(jax.random.uniform(splits[2], (LAYER_NUMBER, PATCH_TOTAL, PATCH_POINTS), jnp.float32, -0.45, 0.45) * steps_of(splits[2], (LAYER_NUMBER, PATCH_TOTAL, PATCH_POINTS), ((1, 128),), -0.4, 0.0), -0.45, 0.45),
        "meridional_current_rate": jnp.clip(jax.random.uniform(splits[3], (LAYER_NUMBER, PATCH_TOTAL, PATCH_POINTS), jnp.float32, -0.45, 0.45) * steps_of(splits[3], (LAYER_NUMBER, PATCH_TOTAL, PATCH_POINTS), ((1, 128),), -0.4, 0.0), -0.45, 0.45),
        "interface_mixing_factor": jnp.clip(jnp.exp(math.log(10.0) - 4.6051702 * jax.random.uniform(splits[4], (LAYER_NUMBER - 1, PATCH_TOTAL, PATCH_POINTS), jnp.float32) ** steps_of(splits[4], (LAYER_NUMBER - 1, PATCH_TOTAL, PATCH_POINTS), ((1, 128),), -0.2, 0.2)), 0.1, 10.0),
        "free_surface_diagonal_term": jnp.clip(jnp.exp(math.log(0.5) - 3.218876 * jax.random.uniform(splits[5], (PATCH_TOTAL, PATCH_POINTS), jnp.float32) ** steps_of(splits[5], (PATCH_TOTAL, PATCH_POINTS), ((0, 128),), -0.2, 0.2)), 0.02, 0.5),
        "surface_drive_source": normal_values(splits[6], (PATCH_TOTAL, PATCH_POINTS), 1.0, 6.0, ((0, 128),), jnp.float32),
        "ocean_patch_flags": draw_ocean_patch_flags(jax.random.fold_in(splits[9], 71), 0),
        "adjacent_patch_indices": draw_adjacent_patch_indices(jax.random.fold_in(splits[9], 71), 0),
    }


def edge_strips(values, with_corners):
    square = values.reshape(values.shape[:-1] + (BSIDE, BSIDE))
    pieces = [square[..., :, -1], square[..., :, 0], square[..., -1, :], square[..., 0, :]]
    if with_corners:
        pieces = pieces + [square[..., -1, -1:], square[..., -1, :1], square[..., 0, -1:], square[..., 0, :1]]
    return jnp.concatenate(pieces, axis=-1)


def pick_borders(strips, source, present):
    def picked(column, start, length):
        taken = jnp.take(strips, source[:, column], axis=-2)[..., start:start + length]
        return jnp.where(present[:, column:column + 1], taken, 0.0)

    borders = [picked(0, BSIDE, BSIDE), picked(1, 0, BSIDE), picked(2, 3 * BSIDE, BSIDE), picked(3, 2 * BSIDE, BSIDE)]
    if strips.shape[-1] > 4 * BSIDE:
        borders = borders + [picked(4, 4 * BSIDE + 3, 1), picked(5, 4 * BSIDE + 2, 1), picked(6, 4 * BSIDE + 1, 1), picked(7, 4 * BSIDE, 1)]
    return borders


def cell_positions(length):
    indices = jnp.arange(length)
    return indices % BSIDE, indices // BSIDE


def across(border):
    return jnp.tile(border, (1,) * (border.ndim - 1) + (BSIDE,))


def along_rows(border):
    return jnp.repeat(border, BSIDE, axis=-1)


def adjacent(values, borders):
    col_index, row_index = cell_positions(values.shape[-1])
    east_side = jnp.where(col_index == BSIDE - 1, along_rows(borders[0]), jnp.roll(values, -1, axis=-1))
    west_side = jnp.where(col_index == 0, along_rows(borders[1]), jnp.roll(values, 1, axis=-1))
    north_side = jnp.where(row_index == BSIDE - 1, across(borders[2]), jnp.roll(values, -BSIDE, axis=-1))
    south_side = jnp.where(row_index == 0, across(borders[3]), jnp.roll(values, BSIDE, axis=-1))
    return east_side, west_side, north_side, south_side


def upwind(carried_quantity, zonal, meridional, beside):
    east_side, west_side, north_side, south_side = beside
    across_x = jnp.maximum(zonal, 0.0) * (carried_quantity - west_side) + jnp.minimum(zonal, 0.0) * (east_side - carried_quantity)
    across_y = jnp.maximum(meridional, 0.0) * (carried_quantity - south_side) + jnp.minimum(meridional, 0.0) * (north_side - carried_quantity)
    return carried_quantity - across_x - across_y


def nine_point(values, diagonal, borders):
    east_side, west_side, north_side, south_side = adjacent(values, borders)
    col_index, row_index = cell_positions(values.shape[-1])
    paired = east_side + west_side
    north_line = jnp.concatenate([borders[2][..., 1:], borders[4]], axis=-1) + jnp.concatenate([borders[5], borders[2][..., :-1]], axis=-1)
    south_line = jnp.concatenate([borders[3][..., 1:], borders[6]], axis=-1) + jnp.concatenate([borders[7], borders[3][..., :-1]], axis=-1)
    upper = jnp.where(row_index == BSIDE - 1, across(north_line), jnp.roll(paired, -BSIDE, axis=-1))
    lower = jnp.where(row_index == 0, across(south_line), jnp.roll(paired, BSIDE, axis=-1))
    return (6.0 + diagonal) * values - (east_side + west_side + north_side + south_side) - 0.5 * (upper + lower)


def vertical_mix(values, interface_mixing_factor):
    levels = values.shape[0]
    factors = []
    carried = []
    for level in range(levels):
        lower_rate = interface_mixing_factor[level - 1] if level > 0 else 0.0
        upper_rate = interface_mixing_factor[level] if level < levels - 1 else 0.0
        pivot = 1.0 + lower_rate + upper_rate
        right_side = values[level]
        if level > 0:
            pivot = pivot - lower_rate * factors[-1]
            right_side = right_side + lower_rate * carried[-1]
        factors.append(upper_rate / pivot)
        carried.append(right_side / pivot)
    solved = [carried[-1]]
    for level in range(levels - 2, -1, -1):
        solved.insert(0, carried[level] + factors[level] * solved[0])
    return jnp.stack(solved)


def reference(potential_heat_value, saltiness_anomaly, zonal_current_rate, meridional_current_rate, interface_mixing_factor, free_surface_diagonal_term, surface_drive_source, ocean_patch_flags, adjacent_patch_indices):
    present = adjacent_patch_indices >= 0
    source = jnp.maximum(adjacent_patch_indices, 0).astype(jnp.int32)
    weight = (ocean_patch_flags > 0).astype(jnp.float32)[:, None]
    mixed_fields = []
    for carried_quantity in (potential_heat_value, saltiness_anomaly, zonal_current_rate, meridional_current_rate):
        borders = pick_borders(edge_strips(carried_quantity, False), source, present)
        advected = upwind(carried_quantity, zonal_current_rate, meridional_current_rate, adjacent(carried_quantity, borders))
        mixed_fields.append(vertical_mix(advected, interface_mixing_factor))
    surface_load = (surface_drive_source + jnp.mean(mixed_fields[0] - mixed_fields[1], axis=0)) * weight
    centre = 6.0 + free_surface_diagonal_term

    def operator(direction):
        return nine_point(direction, free_surface_diagonal_term, pick_borders(edge_strips(direction, True), source, present)) * weight

    height = jnp.zeros_like(surface_load)
    residual = surface_load
    scaled = residual / centre
    direction = scaled
    current = jnp.sum(residual * scaled)
    for iteration in range(ITERS):
        image = operator(direction)
        alpha_step = current / jnp.sum(direction * image)
        height = height + alpha_step * direction
        residual = residual - alpha_step * image
        scaled = residual / centre
        following = jnp.sum(residual * scaled)
        direction = scaled + (following / current) * direction
        current = following
    beside = adjacent(height, pick_borders(edge_strips(height, False), source, present))
    slope_x = 0.5 * (beside[0] - beside[1])
    slope_y = 0.5 * (beside[2] - beside[3])
    return (mixed_fields[0] * weight, mixed_fields[1] * weight, (mixed_fields[2] - slope_x) * weight, (mixed_fields[3] - slope_y) * weight, height * weight)
```

```python
import functools

import jax
import jax.numpy as jnp
from jax import lax
from jax.experimental import pallas as pl
from jax.experimental.pallas import tpu as pltpu
from jax.sharding import PartitionSpec as P

MESH = pl.DeviceIdType.MESH
F32 = jnp.float32
LANES = 128
SLOTS = 8
LEVELS = 8
PAIRS = 32
CELLS = 4096
ROWS = 64
HALO = 4
NEAR = 8


def tile(t):
    return pl.ds(pl.multiple_of(t * LANES, LANES), LANES)


def kernel(
    sizes,
    t_in, s_in, u_in, v_in, k_in, c_in, g_in, flags, lists,
    t_out, s_out, u_out, v_out, sx_out, sy_out, h_out,
    q, kk, cc, src, own_lists, mixed, ip, fu, gl, hx,
    strips, arrived, mstrips, marrived, zstrips, zarrived,
    z2, mi2, zx, mx, mrow, vp, part, near_a, far_a, near_b, far_b,
    in_sem, out_sem, strip_send, strip_recv, m_send, m_recv, z_send, z_recv,
    near_send, near_recv, far_send, far_recv,
):
    count_x, count_y = sizes
    total = count_x * count_y
    gx, gy = lax.axis_index("gx"), lax.axis_index("gy")
    pos = gx * count_y + gy
    far_count = total // NEAR
    highs = count_y // NEAR
    low, high = gy % NEAR, gy // NEAR
    far_id = gx * highs + high
    before, after = (pos + total - 1) % total, (pos + 1) % total
    ring = [(before // count_y, before % count_y), (after // count_y, after % count_y)]
    near_peers = [(gx, high * NEAR + (low + r) % NEAR) for r in range(1, NEAR)]
    far_peers = []
    for r in range(1, far_count):
        other = (far_id + r) % far_count
        far_peers.append((other // highs, (other % highs) * NEAR + low))

    barrier = pltpu.get_barrier_semaphore()
    partners = ring + near_peers + far_peers
    for peer in partners:
        pl.semaphore_signal(barrier, inc=1, device_id=peer, device_id_type=MESH)

    loads = []
    for number, ref in enumerate((t_in, s_in, u_in, v_in)):
        loads.append(
            pltpu.make_async_copy(ref, q.at[number, :, pl.ds(LANES, CELLS)], in_sem.at[number])
        )
    loads.append(pltpu.make_async_copy(lists.at[pl.ds(pos * SLOTS, SLOTS)], own_lists, in_sem.at[4]))
    loads.append(pltpu.make_async_copy(c_in, cc, in_sem.at[5]))
    loads.append(pltpu.make_async_copy(k_in, kk, in_sem.at[6]))
    loads.append(pltpu.make_async_copy(g_in, src, in_sem.at[7]))
    for load in loads:
        load.start()

    lane = lax.broadcasted_iota(jnp.int32, (SLOTS, LANES), 1)
    slot = lax.broadcasted_iota(jnp.int32, (SLOTS, LANES), 0)
    low_half = lane < ROWS
    lane_all = lax.broadcasted_iota(jnp.int32, (LEVELS * SLOTS, LANES), 1)
    weight = jnp.zeros((SLOTS, LANES), F32)
    for b in range(SLOTS):
        flag = jnp.where(flags[pos * SLOTS + b] > 0, 1.0, 0.0)
        weight = jnp.where(slot == b, flag, weight)

    def send_strips(number):
        copies = []
        for side in range(2):
            copy = pltpu.make_async_remote_copy(
                src_ref=strips.at[number],
                dst_ref=arrived.at[1 - side, number],
                send_sem=strip_send.at[side, number],
                recv_sem=strip_recv.at[1 - side, number],
                device_id=ring[side],
                device_id_type=MESH,
            )
            copy.start()
            copies.append(copy)
        return copies

    strip_copies = []
    for number in range(4):
        loads[number].wait()

        def pack(t, acc, number=number):
            moved = pltpu.roll(q[number, :, tile(t + 1)], 2 * t, 1)
            return jnp.where((((lane_all + 1) & 63) >> 1) == t, moved, acc)

        packed = lax.fori_loop(0, PAIRS, pack, jnp.zeros((LEVELS * SLOTS, LANES), F32), unroll=4)
        strips[number, 0] = packed
        strips[number, 1] = jnp.where(
            lane_all < ROWS, q[number, :, tile(1)], q[number, :, tile(PAIRS)]
        )
        if number == 0:
            pl.semaphore_wait(barrier, len(partners))
        strip_copies.append(send_strips(number))

    loads[4].wait()
    loads[5].wait()

    def wide_strips(value, t, store):
        moved = pltpu.roll(value, (8 * t) % ROWS, 1)
        store[t // 8] = jnp.where((((lane + 4) & 63) >> 3) == t % 8, moved, store[t // 8])

    mstrips[...] = jnp.zeros_like(mstrips)

    def diagonal(t, _):
        centre = 6.0 + cc[:, tile(t)]
        inverse = weight / centre
        mi2[t] = inverse
        wide_strips(inverse, t, mstrips)
        mrow[2 * t] = jnp.where(low_half, centre, 0.0)
        mrow[2 * t + 1] = jnp.where(low_half, pltpu.roll(centre, 64, 1), 0.0)
        return 0

    lax.fori_loop(0, PAIRS, diagonal, 0, unroll=2)
    for place, t in enumerate((0, 1, PAIRS - 2, PAIRS - 1)):
        mstrips[4 + place] = mi2[t]

    def exchange(store, landing, send_sem, recv_sem):
        copies = []
        for side in range(2):
            copy = pltpu.make_async_remote_copy(
                src_ref=store,
                dst_ref=landing.at[1 - side],
                send_sem=send_sem.at[side],
                recv_sem=recv_sem.at[1 - side],
                device_id=ring[side],
                device_id_type=MESH,
            )
            copy.start()
            copies.append(copy)
        return copies

    m_copies = exchange(mstrips, marrived, m_send, m_recv)

    listed = own_lists[...]
    relative = (listed - (pos - 1) * SLOTS + total * SLOTS) % (total * SLOTS)
    chosen = []
    for direction in range(8):
        column = jnp.broadcast_to(relative[:, direction : direction + 1], (SLOTS, LANES))
        there = jnp.broadcast_to(listed[:, direction : direction + 1], (SLOTS, LANES)) >= 0
        which = column // SLOTS
        row = jnp.where(there, column % SLOTS, 0)
        chosen.append((row, [there & (which == side) for side in range(3)]))

    def take(direction, sources):
        row, sides = chosen[direction]
        result = jnp.zeros((SLOTS, LANES), F32)
        for source, side in zip(sources, sides):
            result = jnp.where(side, jnp.take_along_axis(source, row, axis=0), result)
        return result

    loads[6].wait()

    def factor(t, _):
        above = None
        for level in range(LEVELS):
            rows = pl.ds(level * SLOTS, SLOTS)
            pivot = 1.0
            if level > 0:
                lower = kk[pl.ds((level - 1) * SLOTS, SLOTS), tile(t)]
                pivot = pivot + lower
            if level < LEVELS - 1:
                upper = kk[rows, tile(t)]
                pivot = pivot + upper
            if level > 0:
                pivot = pivot - lower * above
            inverse = 1.0 / pivot
            ip[rows, tile(t)] = inverse
            if level > 0:
                gl[rows, tile(t)] = lower * inverse
            if level < LEVELS - 1:
                above = upper * inverse
                fu[rows, tile(t)] = above
        return 0

    lax.fori_loop(0, PAIRS, factor, 0)
    loads[7].wait()

    def fill_halos(number):
        for copy in strip_copies[number]:
            copy.wait()

        def fill(level, _):
            rows = pl.ds(pl.multiple_of(level * SLOTS, SLOTS), SLOTS)
            sides = [arrived[0, number, 0, rows], strips[number, 0, rows], arrived[1, number, 0, rows]]
            east = pltpu.roll(take(0, sides), 63, 1)
            west = pltpu.roll(take(1, sides), 65, 1)
            hx[number, rows] = jnp.where((lane & 1) == 1, east, west)
            ends = [arrived[0, number, 1, rows], strips[number, 1, rows], arrived[1, number, 1, rows]]
            end = jnp.where(low_half, take(2, ends), take(3, ends))
            q[number, rows, tile(0)] = end
            q[number, rows, tile(PAIRS + 1)] = end
            return 0

        lax.fori_loop(0, LEVELS, fill, 0)

    east_edge = (lane & 63) == 63
    west_edge = (lane & 63) == 0

    def advance(numbers, t):
        carried = {number: [] for number in numbers}
        for level in range(LEVELS):
            rows = pl.ds(level * SLOTS, SLOTS)
            zonal = q[2, rows, tile(t + 1)]
            meridional = q[3, rows, tile(t + 1)]
            from_west = zonal > 0.0
            from_south = meridional > 0.0
            speed_x = jnp.abs(zonal)
            speed_y = jnp.abs(meridional)
            stay = 1.0 - speed_x - speed_y
            inverse = ip[rows, tile(t)]
            for number in numbers:
                here = q[number, rows, tile(t + 1)]
                edge = pltpu.roll(hx[number, rows], (LANES - 2 * t) % LANES, 1)
                east = jnp.where(east_edge, edge, pltpu.roll(here, LANES - 1, 1))
                west = jnp.where(west_edge, edge, pltpu.roll(here, 1, 1))
                north = pltpu.roll(jnp.where(low_half, q[number, rows, tile(t + 2)], here), 64, 1)
                south = pltpu.roll(jnp.where(low_half, here, q[number, rows, tile(t)]), 64, 1)
                moved = (
                    stay * here
                    + speed_x * jnp.where(from_west, west, east)
                    + speed_y * jnp.where(from_south, south, north)
                )
                value = moved * inverse
                if level > 0:
                    value = value + gl[rows, tile(t)] * carried[number][-1]
                carried[number].append(value)
        solved = {}
        for number in numbers:
            values = carried[number]
            for level in range(LEVELS - 2, -1, -1):
                rows = pl.ds(level * SLOTS, SLOTS)
                values[level] = values[level] + fu[rows, tile(t)] * values[level + 1]
            for level in range(LEVELS):
                mixed[number, pl.ds(level * SLOTS, SLOTS), tile(t)] = values[level] * weight
            solved[number] = values
        return solved

    outs = (t_out, s_out, u_out, v_out)

    def write_out(number):
        copy = pltpu.make_async_copy(mixed.at[number], outs[number], out_sem.at[number])
        copy.start()
        return copy

    fill_halos(0)
    fill_halos(1)
    zstrips[...] = jnp.zeros_like(zstrips)

    def tracers(t, _):
        solved = advance((0, 1), t)
        gap = solved[0][0] - solved[1][0]
        for level in range(1, LEVELS):
            gap = gap + (solved[0][level] - solved[1][level])
        load = src[:, tile(t)] + gap * (1.0 / LEVELS)
        scaled = load * mi2[t]
        z2[t] = scaled
        wide_strips(scaled, t, zstrips)
        return 0

    lax.fori_loop(0, PAIRS, tracers, 0)
    for place, t in enumerate((0, 1, PAIRS - 2, PAIRS - 1)):
        zstrips[4 + place] = z2[t]
    z_copies = exchange(zstrips, zarrived, z_send, z_recv)
    out_copies = [write_out(0), write_out(1)]

    def share(phase, landing, mine, own, peers, send_sem, recv_sem):
        landing[own] = mine[...]
        copies = []
        for r, peer in enumerate(peers, 1):
            copy = pltpu.make_async_remote_copy(
                src_ref=mine,
                dst_ref=landing.at[own],
                send_sem=send_sem.at[phase, r],
                recv_sem=recv_sem.at[phase, own],
                device_id=peer,
                device_id_type=MESH,
            )
            copy.start()
            copies.append(copy)
        return copies

    def gather_sum(phase, copies, landing, mine, own, count, recv_sem):
        for r, copy in enumerate(copies, 1):
            copy.wait_send()
            sender = (own + count - r) % count
            pltpu.make_async_remote_copy(
                src_ref=mine,
                dst_ref=landing.at[sender],
                send_sem=recv_sem.at[phase, sender],
                recv_sem=recv_sem.at[phase, sender],
                device_id=ring[0],
                device_id_type=MESH,
            ).wait_recv()
        result = landing[0]
        for i in range(1, count):
            result = result + landing[i]
        return result

    def gathered(values):
        result = jnp.zeros((SLOTS, LANES), F32)
        for place, value in enumerate(values):
            result = jnp.where(slot == place, jnp.sum(value, axis=0, keepdims=True), result)
        return result

    zero = jnp.zeros((SLOTS, LANES), F32)

    def split(t, carry):
        last, line, norm, product = carry
        value = z2[t]
        for row, moved in ((2 * t, value), (2 * t + 1, pltpu.roll(value, 64, 1))):
            here = jnp.where(low_half, moved, 0.0)
            zx[row + HALO] = here
            ahead = pltpu.roll(here, LANES - 1, 1)
            wide = here + 0.5 * (ahead + pltpu.roll(here, 1, 1))
            norm = norm + here * here * mrow[row]
            product = product + (here * ahead + last * wide)
            last = here
        return last, line, norm, product

    _, _, norm, product = lax.fori_loop(0, PAIRS, split, (zero, zero, zero, zero), unroll=2)
    part[0] = gathered([norm, 2.0 * product])
    copies = share(0, near_a, part.at[0], low, near_peers, near_send, near_recv)

    fill_halos(2)
    fill_halos(3)

    def zonal_step(t, _):
        advance((2,), t)
        return 0

    lax.fori_loop(0, PAIRS, zonal_step, 0)
    out_copies.append(write_out(2))
    part[1] = gather_sum(0, copies, near_a, part.at[0], low, NEAR, near_recv)
    copies = share(0, far_a, part.at[1], far_id, far_peers, far_send, far_recv)

    def meridional_step(t, _):
        advance((3,), t)
        return 0

    lax.fori_loop(0, PAIRS, meridional_step, 0)
    out_copies.append(write_out(3))

    def widen(store, landing, halves, wide, interior):
        def sources(place):
            return [landing[0, place], store[place], landing[1, place]]

        for first, directions, places in (
            (0, (3, 6, 7), (6, 7)),
            (HALO + ROWS, (2, 4, 5), (4, 5)),
        ):
            for i, place in enumerate(places):
                line = take(directions[0], sources(place))
                corner = jnp.where(
                    (lane & 63) < 32,
                    take(directions[1], sources(place)),
                    take(directions[2], sources(place)),
                )
                wide[first + 2 * i] = jnp.where(low_half, line, pltpu.roll(corner, 64, 1))
                wide[first + 2 * i + 1] = jnp.where(low_half, pltpu.roll(line, 64, 1), corner)
        for group in range(4):
            halves[group] = jnp.where(
                (lane & 4) == 0, take(0, sources(group)), take(1, sources(group))
            )

        def rows(t, _):
            side = halves[t // 8]
            step = (8 * t) % ROWS
            even, odd = interior(t)
            wide[HALO + 2 * t] = jnp.where(low_half, even, pltpu.roll(side, 64 - step, 1))
            wide[HALO + 2 * t + 1] = jnp.where(
                low_half, odd, pltpu.roll(side, (LANES - step) % LANES, 1)
            )
            return 0

        lax.fori_loop(0, PAIRS, rows, 0, unroll=2)

    for copy in m_copies:
        copy.wait()
    widen(mstrips, marrived, vp.at[0], mx, lambda t: (mi2[t], pltpu.roll(mi2[t], 64, 1)))
    for copy in z_copies:
        copy.wait()
    widen(
        zstrips, zarrived, vp.at[0], zx,
        lambda t: (zx[HALO + 2 * t], zx[HALO + 2 * t + 1]),
    )

    both = gather_sum(0, copies, far_a, part.at[1], far_id, far_count, far_recv)
    both = jnp.sum(both, axis=1, keepdims=True)
    shift = jnp.broadcast_to(both[1:2] / both[0:1], (SLOTS, LANES))

    def neighbours(value):
        paired = pltpu.roll(value, 1, 1) + pltpu.roll(value, LANES - 1, 1)
        return paired, value + 0.5 * paired

    basis = [zx, vp.at[0], vp.at[1], vp.at[2], vp.at[3]]
    moments = []
    for power in range(4):
        old, new = basis[power], basis[power + 1]
        first, last = 1 + power, HALO + ROWS + 2 - power

        def advance_row(a, carry, old=old, new=new):
            here, paired, wide, behind = carry
            ahead = old[a + 1]
            ahead_paired, ahead_wide = neighbours(ahead)
            value = mx[a] * (paired + behind + ahead_wide) - shift * here
            new[a] = value
            return (ahead, ahead_paired, ahead_wide, wide), here, value

        behind = old[first - 1]
        here = old[first]
        carry = (here, *neighbours(here), neighbours(behind)[1])
        for a in range(first, HALO):
            carry, _, _ = advance_row(a, carry)

        def inner(r, state):
            carry, same, cross = state
            carry, here, value = advance_row(r + HALO, carry)
            centre = mrow[r]
            return carry, same + here * (centre * here), cross + here * (centre * value)

        carry, same, cross = lax.fori_loop(0, ROWS, inner, (carry, zero, zero), unroll=4)
        moments += [same, cross]
        for a in range(HALO + ROWS, last + 1):
            carry, _, _ = advance_row(a, carry)

    part[2] = gathered(moments)
    copies = share(1, near_b, part.at[2], low, near_peers, near_send, near_recv)
    part[3] = gather_sum(1, copies, near_b, part.at[2], low, NEAR, near_recv)
    copies = share(1, far_b, part.at[3], far_id, far_peers, far_send, far_recv)
    sums = gather_sum(1, copies, far_b, part.at[3], far_id, far_count, far_recv)
    sums = jnp.sum(sums, axis=1, keepdims=True)

    mu = [jnp.broadcast_to(sums[i : i + 1], (SLOTS, LANES)) for i in range(8)]
    rest = 1.0 - shift
    matrix = [[rest * mu[i + j] - mu[i + j + 1] for j in range(4)] for i in range(4)]
    lower = [[None] * 4 for _ in range(4)]
    pivots, inverses, ahead = [], [], []
    for j in range(4):
        pivot = matrix[j][j]
        for i in range(j):
            pivot = pivot - lower[j][i] * lower[j][i] * pivots[i]
        kept = pivot > 1e-6 * matrix[j][j]
        pivots.append(jnp.where(kept, pivot, 0.0) if j else pivot)
        inverses.append(jnp.where(kept, 1.0 / pivot, 0.0) if j else 1.0 / pivot)
        for i in range(j + 1, 4):
            entry = matrix[i][j]
            for m in range(j):
                entry = entry - lower[i][m] * lower[j][m] * pivots[m]
            lower[i][j] = entry * inverses[j]
        right = mu[j]
        for i in range(j):
            right = right - lower[j][i] * ahead[i]
        ahead.append(right)
    factors = [None] * 4
    for j in range(3, -1, -1):
        value = ahead[j] * inverses[j]
        for i in range(j + 1, 4):
            value = value - lower[i][j] * factors[i]
        factors[j] = value

    def level_row(a):
        value = factors[0] * basis[0][a]
        for j in range(1, 4):
            value = value + factors[j] * basis[j][a]
        return value

    def slopes(t, carry):
        behind, here = carry
        ahead = level_row(HALO + 2 * t + 1)
        beyond = level_row(HALO + 2 * t + 2)

        def zonal_slope(value):
            return 0.5 * (pltpu.roll(value, LANES - 1, 1) - pltpu.roll(value, 1, 1))

        def joined(even, odd):
            return jnp.where(low_half, even, pltpu.roll(odd, 64, 1))

        sx_out[:, tile(t)] = joined(zonal_slope(here), zonal_slope(ahead))
        sy_out[:, tile(t)] = joined(0.5 * (ahead - behind), 0.5 * (beyond - here))
        h_out[:, tile(t)] = joined(here, ahead)
        return ahead, beyond

    lax.fori_loop(0, PAIRS, slopes, (level_row(HALO - 1), level_row(HALO)), unroll=2)
    for copy in out_copies:
        copy.wait()


def finish_kernel(t_in, s_in, u_in, v_in, sx, sy, h, t_out, s_out, u_out, v_out, h_out):
    t_out[...] = t_in[...]
    s_out[...] = s_in[...]
    h_out[...] = h[...]
    for level in range(LEVELS):
        rows = pl.ds(level * SLOTS, SLOTS)
        u_out[rows] = u_in[rows] - sx[...]
        v_out[rows] = v_in[rows] - sy[...]


def finish(fields, extras, chunks=4):
    width = CELLS // chunks
    wide = pl.BlockSpec((LEVELS * SLOTS, width), lambda i: (0, i))
    thin = pl.BlockSpec((SLOTS, width), lambda i: (0, i))
    big = jax.ShapeDtypeStruct((LEVELS * SLOTS, CELLS), F32)
    small = jax.ShapeDtypeStruct((SLOTS, CELLS), F32)
    return pl.pallas_call(
        finish_kernel,
        grid=(chunks,),
        in_specs=[wide] * 4 + [thin] * 3,
        out_specs=[wide] * 4 + [thin],
        out_shape=[big] * 4 + [small],
        name="finish",
    )(*fields, *extras)


def local(sizes, t, s, u, v, k, c, g, flags, lists):
    stacked = LEVELS * SLOTS
    fields = [x.reshape(stacked, CELLS) for x in (t, s, u, v)]
    big = jax.ShapeDtypeStruct((stacked, CELLS), F32)
    small = jax.ShapeDtypeStruct((SLOTS, CELLS), F32)
    anywhere = pl.BlockSpec(memory_space=pl.ANY)
    vmem = pl.BlockSpec(memory_space=pltpu.VMEM)
    dma = pltpu.SemaphoreType.DMA
    far_count = sizes[0] * sizes[1] // NEAR
    tall = ROWS + 2 * HALO
    results = pl.pallas_call(
        functools.partial(kernel, sizes),
        out_shape=[big] * 4 + [small] * 3,
        in_specs=[anywhere] * 7 + [pl.BlockSpec(memory_space=pltpu.SMEM), anywhere],
        out_specs=[anywhere] * 4 + [vmem] * 3,
        scratch_shapes=[
            pltpu.VMEM((4, stacked, CELLS + 2 * LANES), F32),
            pltpu.VMEM((stacked - SLOTS, CELLS), F32),
            pltpu.VMEM((SLOTS, CELLS), F32),
            pltpu.VMEM((SLOTS, CELLS), F32),
            pltpu.VMEM((SLOTS, 8), jnp.int32),
            pltpu.VMEM((4, stacked, CELLS), F32),
            pltpu.VMEM((stacked, CELLS), F32),
            pltpu.VMEM((stacked, CELLS), F32),
            pltpu.VMEM((stacked, CELLS), F32),
            pltpu.VMEM((4, stacked, LANES), F32),
            pltpu.VMEM((4, 2, stacked, LANES), F32),
            pltpu.VMEM((2, 4, 2, stacked, LANES), F32),
            pltpu.VMEM((8, SLOTS, LANES), F32),
            pltpu.VMEM((2, 8, SLOTS, LANES), F32),
            pltpu.VMEM((8, SLOTS, LANES), F32),
            pltpu.VMEM((2, 8, SLOTS, LANES), F32),
            pltpu.VMEM((PAIRS, SLOTS, LANES), F32),
            pltpu.VMEM((PAIRS, SLOTS, LANES), F32),
            pltpu.VMEM((tall, SLOTS, LANES), F32),
            pltpu.VMEM((tall, SLOTS, LANES), F32),
            pltpu.VMEM((ROWS, SLOTS, LANES), F32),
            pltpu.VMEM((4, tall, SLOTS, LANES), F32),
            pltpu.VMEM((4, SLOTS, LANES), F32),
            pltpu.VMEM((NEAR, SLOTS, LANES), F32),
            pltpu.VMEM((far_count, SLOTS, LANES), F32),
            pltpu.VMEM((NEAR, SLOTS, LANES), F32),
            pltpu.VMEM((far_count, SLOTS, LANES), F32),
            dma((8,)),
            dma((4,)),
            dma((2, 4)),
            dma((2, 4)),
            dma((2,)),
            dma((2,)),
            dma((2,)),
            dma((2,)),
            dma((2, NEAR)),
            dma((2, NEAR)),
            dma((2, far_count)),
            dma((2, far_count)),
        ],
        compiler_params=pltpu.CompilerParams(
            collective_id=0, has_side_effects=True, vmem_limit_bytes=40 * 1024 * 1024
        ),
        name="ocean_step",
    )(*fields, k.reshape(stacked - SLOTS, CELLS), c, g, flags, lists)
    done = finish(results[:4], results[4:])
    shape = (LEVELS, SLOTS, CELLS)
    return tuple(x.reshape(shape) for x in done[:4]) + (done[4],)


def solution(mesh):
    whole = P(None, ("gx", "gy"), None)
    flat = P(("gx", "gy"), None)
    return jax.shard_map(
        functools.partial(local, (mesh.shape["gx"], mesh.shape["gy"])),
        mesh=mesh,
        in_specs=(whole, whole, whole, whole, whole, flat, flat, P(), P()),
        out_specs=(whole, whole, whole, whole, flat),
        check_vma=False,
    )
```

```python
import functools

import jax
import jax.numpy as jnp
from jax import lax
from jax.experimental import pallas as pl
from jax.experimental.pallas import tpu as pltpu
from jax.sharding import PartitionSpec as P

MESH = pl.DeviceIdType.MESH
F32 = jnp.float32
BF16 = jnp.bfloat16
LANES = 128
SLOTS = 8
LEVELS = 8
PAIRS = 32
CELLS = 4096
ROWS = 64
HALO = 4
CHUNK = 8
NEAR = 8


def tile(t):
    return pl.ds(pl.multiple_of(t * LANES, LANES), LANES)


def kernel(
    sizes,
    t_in, s_in, u_in, v_in, k_in, c_in, g_in, flags_in, lists,
    t_out, s_out, u_out, v_out, sx_out, sy_out, h_out,
    q, kk, cc, src, own_lists, flags, mixed, ip, fu, gl, hx,
    east_of, west_of, half_of, edge_of, shifts, spread,
    strips, arrived, mstrips, marrived, zstrips, zarrived,
    z2, mi2, zx, mx, mrow, v1, v2, v3, v4, part, near_a, far_a, near_b, far_b,
    in_sem, out_sem, strip_send, strip_recv, m_send, m_recv, z_send, z_recv,
    near_send, near_recv, far_send, far_recv,
):
    count_x, count_y = sizes
    total = count_x * count_y
    gx, gy = lax.axis_index("gx"), lax.axis_index("gy")
    pos = gx * count_y + gy
    far_count = total // NEAR
    highs = count_y // NEAR
    low, high = gy % NEAR, gy // NEAR
    far_id = gx * highs + high
    before, after = (pos + total - 1) % total, (pos + 1) % total
    ring = [(before // count_y, before % count_y), (after // count_y, after % count_y)]
    near_peers = [(gx, high * NEAR + (low + r) % NEAR) for r in range(1, NEAR)]
    far_peers = []
    for r in range(1, far_count):
        other = (far_id + r) % far_count
        far_peers.append((other // highs, (other % highs) * NEAR + low))

    barrier = pltpu.get_barrier_semaphore()
    partners = ring + near_peers + far_peers
    for peer in partners:
        pl.semaphore_signal(barrier, inc=1, device_id=peer, device_id_type=MESH)

    loads = []
    for number, ref in enumerate((t_in, s_in, u_in, v_in)):
        loads.append(
            pltpu.make_async_copy(ref, q.at[number], in_sem.at[number])
        )
    loads.append(pltpu.make_async_copy(
            lists.at[:, tile(pos // (LANES // SLOTS))], own_lists, in_sem.at[4]
        ))
    loads.append(pltpu.make_async_copy(c_in, cc, in_sem.at[5]))
    loads.append(pltpu.make_async_copy(k_in, kk, in_sem.at[6]))
    loads.append(pltpu.make_async_copy(g_in, src, in_sem.at[7]))
    for load in loads:
        load.start()
    flag_load = pltpu.make_async_copy(flags_in, flags, in_sem.at[8])
    flag_load.start()

    lane = lax.broadcasted_iota(jnp.int32, (SLOTS, LANES), 1)
    slot = lax.broadcasted_iota(jnp.int32, (SLOTS, LANES), 0)
    low_half = lane < ROWS
    lane_all = lax.broadcasted_iota(jnp.int32, (LEVELS * SLOTS, LANES), 1)

    def send_strips(number):
        copies = []
        for side in range(2):
            copy = pltpu.make_async_remote_copy(
                src_ref=strips.at[number],
                dst_ref=arrived.at[1 - side, number],
                send_sem=strip_send.at[side, number],
                recv_sem=strip_recv.at[1 - side, number],
                device_id=ring[side],
                device_id_type=MESH,
            )
            copy.start()
            copies.append(copy)
        return copies

    row = lax.broadcasted_iota(jnp.int32, (2 * LANES, LANES), 0) % LANES
    column = lax.broadcasted_iota(jnp.int32, (2 * LANES, LANES), 1)
    odd = column % 2 == 1
    upper_odd = (column >= 63) & (column < 127)
    packing = jnp.where(
        odd, jnp.where(upper_odd, 63, 127), jnp.where(column < ROWS, 0, ROWS)
    )
    edge_row = row % 2 == 1
    target = jnp.where(
        edge_row,
        jnp.where((row >= 63) & (row < 127), 0, ROWS),
        jnp.where(row < ROWS, 63, 127),
    )
    for place, chosen_lanes in enumerate(
        (
            (row == column + 1) & (column % ROWS != ROWS - 1),
            (row == column - 1) & (column % ROWS != 0),
            row == (column + ROWS) % LANES,
            row == packing,
        )
    ):
        shifts[:, place * LANES : (place + 1) * LANES] = jnp.where(chosen_lanes, 1.0, 0.0).astype(BF16)
    spread[...] = jnp.where(column == target, 1.0, 0.0).astype(BF16)

    def parts(value):
        high = value.astype(BF16)
        rest = (value - high.astype(F32)).astype(BF16)
        return jnp.concatenate([high, rest], axis=1)

    stacked = LEVELS * SLOTS
    strip_copies = []
    for number in range(4):
        loads[number].wait()

        def shift_all(chunk, acc, number=number):
            first = chunk * CHUNK
            split_parts = jnp.concatenate(
                [parts(q[number, :, tile(first + i)]) for i in range(CHUNK)], axis=0
            )
            moved = jnp.dot(split_parts, shifts[...], preferred_element_type=F32)
            for i in range(CHUNK):
                rows = slice(i * stacked, (i + 1) * stacked)
                east_of[number, :, tile(first + i)] = moved[rows, :LANES]
                west_of[number, :, tile(first + i)] = moved[rows, LANES : 2 * LANES]
                half_of[number, :, tile(first + i + 1)] = moved[rows, 2 * LANES : 3 * LANES]
                here = (((lane_all + 1) & 63) >> 1) == first + i
                acc = jnp.where(here, moved[rows, 3 * LANES :], acc)
            return acc

        strips[number, 0] = lax.fori_loop(
            0, PAIRS // CHUNK, shift_all, jnp.zeros((stacked, LANES), F32)
        )
        strips[number, 1] = jnp.where(
            lane_all < ROWS, q[number, :, tile(0)], q[number, :, tile(PAIRS - 1)]
        )
        if number == 0:
            pl.semaphore_wait(barrier, len(partners))
        strip_copies.append(send_strips(number))

    flag_load.wait()
    weight = jnp.zeros((SLOTS, LANES), F32)
    for b in range(SLOTS):
        flag = jnp.where(flags[pos * SLOTS + b] > 0, 1.0, 0.0)
        weight = jnp.where(slot == b, flag, weight)

    loads[4].wait()
    loads[5].wait()

    def wide_strips(value_of, store):
        for group in range(4):
            packed = jnp.zeros((SLOTS, LANES), F32)
            for k in range(8):
                value = value_of[8 * group + k]
                moved = pltpu.roll(value, 8 * k, 1) if k else value
                packed = jnp.where((((lane + 4) & 63) >> 3) == k, moved, packed)
            store[group] = packed
        for place, t in enumerate((0, 1, PAIRS - 2, PAIRS - 1)):
            store[4 + place] = value_of[t]

    def diagonal(t, _):
        centre = 6.0 + cc[:, tile(t)]
        mi2[t] = weight / centre
        mrow[2 * t] = jnp.where(low_half, centre, 0.0)
        mrow[2 * t + 1] = jnp.where(low_half, pltpu.roll(centre, 64, 1), 0.0)
        return 0

    lax.fori_loop(0, PAIRS, diagonal, 0, unroll=8)
    wide_strips(mi2, mstrips)

    def exchange(store, landing, send_sem, recv_sem):
        copies = []
        for side in range(2):
            copy = pltpu.make_async_remote_copy(
                src_ref=store,
                dst_ref=landing.at[1 - side],
                send_sem=send_sem.at[side],
                recv_sem=recv_sem.at[1 - side],
                device_id=ring[side],
                device_id_type=MESH,
            )
            copy.start()
            copies.append(copy)
        return copies

    m_copies = exchange(mstrips, marrived, m_send, m_recv)

    listed_lanes = pltpu.roll(
        own_lists[...].astype(F32), (LANES - (pos % (LANES // SLOTS)) * SLOTS) % LANES, 1
    )
    chosen = []
    for direction in range(8):
        line = jnp.broadcast_to(listed_lanes[direction : direction + 1], (SLOTS, LANES))
        own = jnp.sum(jnp.where(lane == slot, line, 0.0), axis=1, keepdims=True)
        listed = jnp.broadcast_to(own, (SLOTS, LANES)).astype(jnp.int32)
        column = (listed - (pos - 1) * SLOTS + total * SLOTS) % (total * SLOTS)
        there = listed >= 0
        which = column // SLOTS
        row = jnp.where(there, column % SLOTS, 0)
        chosen.append((row, [there & (which == side) for side in range(3)]))

    def take(direction, sources):
        row, sides = chosen[direction]
        result = jnp.zeros((SLOTS, LANES), F32)
        for source, side in zip(sources, sides):
            result = jnp.where(side, jnp.take_along_axis(source, row, axis=0), result)
        return result

    loads[6].wait()

    def factor(t, _):
        above = None
        for level in range(LEVELS):
            rows = pl.ds(level * SLOTS, SLOTS)
            pivot = 1.0
            if level > 0:
                lower = kk[pl.ds((level - 1) * SLOTS, SLOTS), tile(t)]
                pivot = pivot + lower
            if level < LEVELS - 1:
                upper = kk[rows, tile(t)]
                pivot = pivot + upper
            if level > 0:
                pivot = pivot - lower * above
            inverse = 1.0 / pivot
            ip[rows, tile(t)] = inverse * weight
            if level > 0:
                gl[rows, tile(t)] = lower * inverse
            if level < LEVELS - 1:
                above = upper * inverse
                fu[rows, tile(t)] = above
        return 0

    lax.fori_loop(0, PAIRS, factor, 0, unroll=2)
    loads[7].wait()

    def fill_halos(number):
        for copy in strip_copies[number]:
            copy.wait()

        for level in range(LEVELS):
            rows = pl.ds(level * SLOTS, SLOTS)
            sides = [arrived[0, number, 0, rows], strips[number, 0, rows], arrived[1, number, 0, rows]]
            hx[number, rows] = jnp.where((lane & 1) == 1, take(1, sides), take(0, sides))
            ends = [arrived[0, number, 1, rows], strips[number, 1, rows], arrived[1, number, 1, rows]]
            end = pltpu.roll(jnp.where(low_half, take(2, ends), take(3, ends)), 64, 1)
            half_of[number, rows, tile(0)] = end
            half_of[number, rows, tile(PAIRS + 1)] = end
        halo_parts = parts(hx[number])

        def edges(chunk, _):
            first = chunk * CHUNK
            position = lax.broadcasted_iota(jnp.int32, (stacked, 2 * LANES), 1)
            pieces = []
            for i in range(CHUNK):
                here = (((position + 1) & 63) >> 1) == first + i
                pieces.append(jnp.where(here, halo_parts, jnp.zeros_like(halo_parts)))
            found = jnp.dot(
                jnp.concatenate(pieces, axis=0), spread[...], preferred_element_type=F32
            )
            for i in range(CHUNK):
                edge_of[number, :, tile(first + i)] = found[i * stacked : (i + 1) * stacked]
            return 0

        lax.fori_loop(0, PAIRS // CHUNK, edges, 0)

    east_edge = (lane & 63) == 63
    west_edge = (lane & 63) == 0

    def advance(numbers, t):
        carried = {number: [] for number in numbers}
        for level in range(LEVELS):
            rows = pl.ds(level * SLOTS, SLOTS)
            zonal = q[2, rows, tile(t)]
            meridional = q[3, rows, tile(t)]
            from_west = zonal > 0.0
            from_south = meridional > 0.0
            outside = (east_edge & jnp.logical_not(from_west)) | (west_edge & from_west)
            behind = low_half & from_south
            beyond = jnp.logical_not(low_half | from_south)
            speed_x = jnp.abs(zonal)
            speed_y = jnp.abs(meridional)
            stay = 1.0 - speed_x - speed_y
            inverse = ip[rows, tile(t)]
            for number in numbers:
                along = jnp.where(from_west, west_of[number, rows, tile(t)], east_of[number, rows, tile(t)])
                along = jnp.where(outside, edge_of[number, rows, tile(t)], along)
                across = jnp.where(beyond, half_of[number, rows, tile(t + 2)], half_of[number, rows, tile(t + 1)])
                across = jnp.where(behind, half_of[number, rows, tile(t)], across)
                moved = stay * q[number, rows, tile(t)] + speed_x * along + speed_y * across
                value = moved * inverse
                if level > 0:
                    value = value + gl[rows, tile(t)] * carried[number][-1]
                carried[number].append(value)
        solved = {}
        for number in numbers:
            values = carried[number]
            for level in range(LEVELS - 2, -1, -1):
                rows = pl.ds(level * SLOTS, SLOTS)
                values[level] = values[level] + fu[rows, tile(t)] * values[level + 1]
            for level in range(LEVELS):
                mixed[number, pl.ds(level * SLOTS, SLOTS), tile(t)] = values[level]
            solved[number] = values
        return solved

    outs = (t_out, s_out, u_out, v_out)

    def write_out(number):
        copy = pltpu.make_async_copy(mixed.at[number], outs[number], out_sem.at[number])
        copy.start()
        return copy

    fill_halos(0)
    fill_halos(1)

    def tracers(t, _):
        solved = advance((0, 1), t)
        gap = solved[0][0] - solved[1][0]
        for level in range(1, LEVELS):
            gap = gap + (solved[0][level] - solved[1][level])
        load = src[:, tile(t)] + gap * (1.0 / LEVELS)
        scaled = load * mi2[t]
        z2[t] = scaled
        return 0

    lax.fori_loop(0, PAIRS, tracers, 0)
    wide_strips(z2, zstrips)
    z_copies = exchange(zstrips, zarrived, z_send, z_recv)
    out_copies = [write_out(0), write_out(1)]

    def share(phase, landing, mine, own, peers, send_sem, recv_sem):
        landing[own] = mine[...]
        copies = []
        for r, peer in enumerate(peers, 1):
            copy = pltpu.make_async_remote_copy(
                src_ref=mine,
                dst_ref=landing.at[own],
                send_sem=send_sem.at[phase, r],
                recv_sem=recv_sem.at[phase, own],
                device_id=peer,
                device_id_type=MESH,
            )
            copy.start()
            copies.append(copy)
        return copies

    def gather_sum(phase, copies, landing, mine, own, count, recv_sem):
        for r, copy in enumerate(copies, 1):
            copy.wait_send()
            sender = (own + count - r) % count
            pltpu.make_async_remote_copy(
                src_ref=mine,
                dst_ref=landing.at[sender],
                send_sem=recv_sem.at[phase, sender],
                recv_sem=recv_sem.at[phase, sender],
                device_id=ring[0],
                device_id_type=MESH,
            ).wait_recv()
        result = landing[0]
        for i in range(1, count):
            result = result + landing[i]
        return result

    def gathered(values):
        result = jnp.zeros((SLOTS, LANES), F32)
        for place, value in enumerate(values):
            result = jnp.where(slot == place, jnp.sum(value, axis=0, keepdims=True), result)
        return result

    zero = jnp.zeros((SLOTS, LANES), F32)

    def split(t, carry):
        last, line, norm, product = carry
        value = z2[t]
        for row, moved in ((2 * t, value), (2 * t + 1, pltpu.roll(value, 64, 1))):
            here = jnp.where(low_half, moved, 0.0)
            zx[row + HALO] = here
            ahead = pltpu.roll(here, LANES - 1, 1)
            wide = here + 0.5 * (ahead + pltpu.roll(here, 1, 1))
            norm = norm + here * here * mrow[row]
            product = product + (here * ahead + last * wide)
            last = here
        return last, line, norm, product

    _, _, norm, product = lax.fori_loop(0, PAIRS, split, (zero, zero, zero, zero), unroll=8)
    part[0] = gathered([norm, 2.0 * product])
    copies = share(0, near_a, part.at[0], low, near_peers, near_send, near_recv)

    fill_halos(2)
    fill_halos(3)

    def zonal_step(t, _):
        advance((2,), t)
        return 0

    lax.fori_loop(0, PAIRS, zonal_step, 0)
    out_copies.append(write_out(2))
    part[1] = gather_sum(0, copies, near_a, part.at[0], low, NEAR, near_recv)
    copies = share(0, far_a, part.at[1], far_id, far_peers, far_send, far_recv)

    def meridional_step(t, _):
        advance((3,), t)
        return 0

    lax.fori_loop(0, PAIRS, meridional_step, 0)
    out_copies.append(write_out(3))

    def widen(store, landing, halves, wide, interior):
        def sources(place):
            return [landing[0, place], store[place], landing[1, place]]

        for first, directions, places in (
            (0, (3, 6, 7), (6, 7)),
            (HALO + ROWS, (2, 4, 5), (4, 5)),
        ):
            for i, place in enumerate(places):
                line = take(directions[0], sources(place))
                corner = jnp.where(
                    (lane & 63) < 32,
                    take(directions[1], sources(place)),
                    take(directions[2], sources(place)),
                )
                wide[first + 2 * i] = jnp.where(low_half, line, pltpu.roll(corner, 64, 1))
                wide[first + 2 * i + 1] = jnp.where(low_half, pltpu.roll(line, 64, 1), corner)
        for group in range(4):
            halves[group] = jnp.where(
                (lane & 4) == 0, take(0, sources(group)), take(1, sources(group))
            )

        def rows(t, _):
            side = halves[t // 8]
            step = (8 * t) % ROWS
            even, odd = interior(t)
            wide[HALO + 2 * t] = jnp.where(low_half, even, pltpu.roll(side, 64 - step, 1))
            wide[HALO + 2 * t + 1] = jnp.where(
                low_half, odd, pltpu.roll(side, (LANES - step) % LANES, 1)
            )
            return 0

        lax.fori_loop(0, PAIRS, rows, 0, unroll=8)

    for copy in m_copies:
        copy.wait()
    widen(mstrips, marrived, v1, mx, lambda t: (mi2[t], pltpu.roll(mi2[t], 64, 1)))
    for copy in z_copies:
        copy.wait()
    widen(
        zstrips, zarrived, v1, zx,
        lambda t: (zx[HALO + 2 * t], zx[HALO + 2 * t + 1]),
    )

    both = gather_sum(0, copies, far_a, part.at[1], far_id, far_count, far_recv)
    both = jnp.sum(both, axis=1, keepdims=True)
    shift = jnp.broadcast_to(both[1:2] / both[0:1], (SLOTS, LANES))

    def neighbours(value):
        paired = pltpu.roll(value, 1, 1) + pltpu.roll(value, LANES - 1, 1)
        return paired, value + 0.5 * paired

    basis = [zx, v1, v2, v3, v4]
    moments = []
    for power in range(4):
        old, new = basis[power], basis[power + 1]
        first, last = 1 + power, HALO + ROWS + 2 - power

        def advance_row(a, carry, old=old, new=new):
            here, paired, wide, behind = carry
            ahead = old[a + 1]
            ahead_paired, ahead_wide = neighbours(ahead)
            value = mx[a] * (paired + behind + ahead_wide) - shift * here
            new[a] = value
            return (ahead, ahead_paired, ahead_wide, wide), here, value

        behind = old[first - 1]
        here = old[first]
        carry = (here, *neighbours(here), neighbours(behind)[1])
        for a in range(first, HALO):
            carry, _, _ = advance_row(a, carry)

        def inner(r, state):
            carry, same, cross = state
            carry, here, value = advance_row(r + HALO, carry)
            centre = mrow[r]
            return carry, same + here * (centre * here), cross + here * (centre * value)

        carry, same, cross = lax.fori_loop(0, ROWS, inner, (carry, zero, zero), unroll=16)
        moments += [same, cross]
        for a in range(HALO + ROWS, last + 1):
            carry, _, _ = advance_row(a, carry)

    part[2] = gathered(moments)
    copies = share(1, near_b, part.at[2], low, near_peers, near_send, near_recv)
    part[3] = gather_sum(1, copies, near_b, part.at[2], low, NEAR, near_recv)
    copies = share(1, far_b, part.at[3], far_id, far_peers, far_send, far_recv)
    sums = gather_sum(1, copies, far_b, part.at[3], far_id, far_count, far_recv)
    sums = jnp.sum(sums, axis=1, keepdims=True)

    mu = [jnp.broadcast_to(sums[i : i + 1], (SLOTS, LANES)) for i in range(8)]
    rest = 1.0 - shift
    matrix = [[rest * mu[i + j] - mu[i + j + 1] for j in range(4)] for i in range(4)]
    lower = [[None] * 4 for _ in range(4)]
    pivots, inverses, ahead = [], [], []
    for j in range(4):
        pivot = matrix[j][j]
        for i in range(j):
            pivot = pivot - lower[j][i] * lower[j][i] * pivots[i]
        kept = pivot > 1e-6 * matrix[j][j]
        pivots.append(jnp.where(kept, pivot, 0.0) if j else pivot)
        inverses.append(jnp.where(kept, 1.0 / pivot, 0.0) if j else 1.0 / pivot)
        for i in range(j + 1, 4):
            entry = matrix[i][j]
            for m in range(j):
                entry = entry - lower[i][m] * lower[j][m] * pivots[m]
            lower[i][j] = entry * inverses[j]
        right = mu[j]
        for i in range(j):
            right = right - lower[j][i] * ahead[i]
        ahead.append(right)
    factors = [None] * 4
    for j in range(3, -1, -1):
        value = ahead[j] * inverses[j]
        for i in range(j + 1, 4):
            value = value - lower[i][j] * factors[i]
        factors[j] = value

    def level_row(a):
        value = factors[0] * basis[0][a]
        for j in range(1, 4):
            value = value + factors[j] * basis[j][a]
        return value

    def slopes(t, carry):
        behind, here = carry
        ahead = level_row(HALO + 2 * t + 1)
        beyond = level_row(HALO + 2 * t + 2)

        def zonal_slope(value):
            return 0.5 * (pltpu.roll(value, LANES - 1, 1) - pltpu.roll(value, 1, 1))

        def joined(even, odd):
            return jnp.where(low_half, even, pltpu.roll(odd, 64, 1))

        sx_out[:, tile(t)] = joined(zonal_slope(here), zonal_slope(ahead))
        sy_out[:, tile(t)] = joined(0.5 * (ahead - behind), 0.5 * (beyond - here))
        h_out[:, tile(t)] = joined(here, ahead)
        return ahead, beyond

    lax.fori_loop(0, PAIRS, slopes, (level_row(HALO - 1), level_row(HALO)), unroll=8)
    for copy in out_copies:
        copy.wait()


def finish_kernel(t_in, s_in, u_in, v_in, sx, sy, h, t_out, s_out, u_out, v_out, h_out):
    t_out[...] = t_in[...]
    s_out[...] = s_in[...]
    h_out[...] = h[...]
    for level in range(LEVELS):
        rows = pl.ds(level * SLOTS, SLOTS)
        u_out[rows] = u_in[rows] - sx[...]
        v_out[rows] = v_in[rows] - sy[...]


def finish(fields, extras, chunks=4):
    width = CELLS // chunks
    wide = pl.BlockSpec((LEVELS * SLOTS, width), lambda i: (0, i))
    thin = pl.BlockSpec((SLOTS, width), lambda i: (0, i))
    big = jax.ShapeDtypeStruct((LEVELS * SLOTS, CELLS), F32)
    small = jax.ShapeDtypeStruct((SLOTS, CELLS), F32)
    return pl.pallas_call(
        finish_kernel,
        grid=(chunks,),
        in_specs=[wide] * 4 + [thin] * 3,
        out_specs=[wide] * 4 + [thin],
        out_shape=[big] * 4 + [small],
        compiler_params=pltpu.CompilerParams(vmem_limit_bytes=16 * 1024 * 1024),
        name="finish",
    )(*fields, *extras)


def local(sizes, t, s, u, v, k, c, g, flags, lists):
    stacked = LEVELS * SLOTS
    fields = [x.reshape(stacked, CELLS) for x in (t, s, u, v)]
    big = jax.ShapeDtypeStruct((stacked, CELLS), F32)
    small = jax.ShapeDtypeStruct((SLOTS, CELLS), F32)
    anywhere = pl.BlockSpec(memory_space=pl.ANY)
    held = pl.BlockSpec(memory_space=pltpu.HBM)
    vmem = pl.BlockSpec(memory_space=pltpu.VMEM)
    dma = pltpu.SemaphoreType.DMA
    far_count = sizes[0] * sizes[1] // NEAR
    tall = ROWS + 2 * HALO
    results = pl.pallas_call(
        functools.partial(kernel, sizes),
        out_shape=[big] * 4 + [small] * 3,
        in_specs=[held] * 9,
        out_specs=[anywhere] * 4 + [vmem] * 3,
        scratch_shapes=[
            pltpu.VMEM((4, stacked, CELLS), F32),
            pltpu.VMEM((stacked - SLOTS, CELLS), F32),
            pltpu.VMEM((SLOTS, CELLS), F32),
            pltpu.VMEM((SLOTS, CELLS), F32),
            pltpu.VMEM((8, LANES), jnp.int32),
            pltpu.SMEM((SLOTS * far_count * NEAR,), jnp.int32),
            pltpu.VMEM((4, stacked, CELLS), F32),
            pltpu.VMEM((stacked, CELLS), F32),
            pltpu.VMEM((stacked, CELLS), F32),
            pltpu.VMEM((stacked, CELLS), F32),
            pltpu.VMEM((4, stacked, LANES), F32),
            pltpu.VMEM((4, stacked, CELLS), F32),
            pltpu.VMEM((4, stacked, CELLS), F32),
            pltpu.VMEM((4, stacked, CELLS + 2 * LANES), F32),
            pltpu.VMEM((4, stacked, CELLS), F32),
            pltpu.VMEM((2 * LANES, 4 * LANES), BF16),
            pltpu.VMEM((2 * LANES, LANES), BF16),
            pltpu.VMEM((4, 2, stacked, LANES), F32),
            pltpu.VMEM((2, 4, 2, stacked, LANES), F32),
            pltpu.VMEM((8, SLOTS, LANES), F32),
            pltpu.VMEM((2, 8, SLOTS, LANES), F32),
            pltpu.VMEM((8, SLOTS, LANES), F32),
            pltpu.VMEM((2, 8, SLOTS, LANES), F32),
            pltpu.VMEM((PAIRS, SLOTS, LANES), F32),
            pltpu.VMEM((PAIRS, SLOTS, LANES), F32),
            pltpu.VMEM((tall, SLOTS, LANES), F32),
            pltpu.VMEM((tall, SLOTS, LANES), F32),
            pltpu.VMEM((ROWS, SLOTS, LANES), F32),
            pltpu.VMEM((tall, SLOTS, LANES), F32),
            pltpu.VMEM((tall, SLOTS, LANES), F32),
            pltpu.VMEM((tall, SLOTS, LANES), F32),
            pltpu.VMEM((tall, SLOTS, LANES), F32),
            pltpu.VMEM((4, SLOTS, LANES), F32),
            pltpu.VMEM((NEAR, SLOTS, LANES), F32),
            pltpu.VMEM((far_count, SLOTS, LANES), F32),
            pltpu.VMEM((NEAR, SLOTS, LANES), F32),
            pltpu.VMEM((far_count, SLOTS, LANES), F32),
            dma((9,)),
            dma((4,)),
            dma((2, 4)),
            dma((2, 4)),
            dma((2,)),
            dma((2,)),
            dma((2,)),
            dma((2,)),
            dma((2, NEAR)),
            dma((2, NEAR)),
            dma((2, far_count)),
            dma((2, far_count)),
        ],
        compiler_params=pltpu.CompilerParams(
            collective_id=0, has_side_effects=True, vmem_limit_bytes=40 * 1024 * 1024
        ),
        name="ocean_step",
    )(
        *[
            pltpu.with_memory_space_constraint(x, pltpu.HBM)
            for x in (*fields, k.reshape(stacked - SLOTS, CELLS), c, g, flags, lists.T)
        ],
    )
    done = finish(results[:4], results[4:])
    shape = (LEVELS, SLOTS, CELLS)
    return tuple(x.reshape(shape) for x in done[:4]) + (done[4],)


def solution(mesh):
    whole = P(None, ("gx", "gy"), None)
    flat = P(("gx", "gy"), None)
    return jax.shard_map(
        functools.partial(local, (mesh.shape["gx"], mesh.shape["gy"])),
        mesh=mesh,
        in_specs=(whole, whole, whole, whole, whole, flat, flat, P(), P()),
        out_specs=(whole, whole, whole, whole, flat),
        check_vma=False,
    )
```

```python
import functools
import itertools

import jax
import jax.numpy as jnp
from jax import lax
from jax.experimental import pallas as pl
from jax.experimental.pallas import tpu as pltpu
from jax.sharding import PartitionSpec as P

MESH = pl.DeviceIdType.MESH
F32 = jnp.float32
BF16 = jnp.bfloat16
LANES = 128
SLOTS = 8
LEVELS = 8
PAIRS = 32
CELLS = 4096
ROWS = 64
HALO = 4
CHUNK = 8
PARTS = 4


def tile(t):
    return pl.ds(pl.multiple_of(t * LANES, LANES), LANES)


def kernel(
    sizes,
    t_in, s_in, u_in, v_in, k_in, c_in, g_in, flags_in, lists,
    t_out, s_out, u_out, v_out, sx_out, sy_out, h_out,
    q, kk, cc, src, own_lists, flags, mixed, ip, fu, gl, hx,
    east_of, west_of, half_of, edge_of, shifts, spread,
    strips, arrived, mstrips, marrived, zstrips, zarrived,
    z2, mi2, zx, mx, mrow, v1, v2, v3, v4, inward, choose, part, near_sums, far_sums,
    in_sem, out_sem, strip_send, strip_recv, m_send, m_recv, z_send, z_recv, sum_send, sum_recv,
):
    count_x, count_y = sizes
    total = count_x * count_y
    gx, gy = lax.axis_index("gx"), lax.axis_index("gy")
    pos = gx * count_y + gy
    before, after = (pos + total - 1) % total, (pos + 1) % total
    ring = [(before // count_y, before % count_y), (after // count_y, after % count_y)]

    ys = [(gx + n) % 4 for n in range(4)]
    zs = [(gy // 8 + n) % 4 * 8 for n in range(4)]
    xs = [(gy // 2 + n) % 4 * 2 for n in range(4)]
    cores = [(gy + n) % 2 for n in range(2)]

    def hops(step):
        return -sum(min(n, 4 - n) for n in step)

    near_steps = sorted(itertools.product((0, 2, 1, 3), range(2)), key=lambda step: hops(step[:1]))
    far_steps = sorted(itertools.product(range(4), range(4)), key=hops)
    near = [(gx, zs[0] + xs[x] + cores[c]) for x, c in near_steps if x or c]
    far = [(ys[y], zs[z] + xs[0] + cores[0]) for y, z in far_steps if y or z]
    groups = ((near, gy % 8), (far, gx * 4 + gy // 8))
    partners = ring + near + far

    barrier = pltpu.get_barrier_semaphore()

    loads = []
    for number, ref in enumerate((t_in, s_in, u_in, v_in)):
        loads.append(pltpu.make_async_copy(ref, q.at[number], in_sem.at[number]))
    loads.append(pltpu.make_async_copy(
            lists.at[:, tile(pos // (LANES // SLOTS))], own_lists, in_sem.at[4]
        ))
    loads.append(pltpu.make_async_copy(c_in, cc, in_sem.at[5]))
    loads.append(pltpu.make_async_copy(k_in, kk, in_sem.at[6]))
    loads.append(pltpu.make_async_copy(g_in, src, in_sem.at[7]))
    for load in loads:
        load.start()
    flag_load = pltpu.make_async_copy(flags_in, flags, in_sem.at[8])
    flag_load.start()
    for other in partners:
        pl.semaphore_signal(barrier, inc=1, device_id=other, device_id_type=MESH)

    lane = lax.broadcasted_iota(jnp.int32, (SLOTS, LANES), 1)
    slot = lax.broadcasted_iota(jnp.int32, (SLOTS, LANES), 0)
    low_half = lane < ROWS
    lane_all = lax.broadcasted_iota(jnp.int32, (LEVELS * SLOTS, LANES), 1)

    def send_strips(number):
        copies = []
        for side in range(2):
            copy = pltpu.make_async_remote_copy(
                src_ref=strips.at[number],
                dst_ref=arrived.at[1 - side, number],
                send_sem=strip_send.at[side, number],
                recv_sem=strip_recv.at[1 - side, number],
                device_id=ring[side],
                device_id_type=MESH,
            )
            copy.start()
            copies.append(copy)
        return copies

    row = lax.broadcasted_iota(jnp.int32, (2 * LANES, LANES), 0) % LANES
    column = lax.broadcasted_iota(jnp.int32, (2 * LANES, LANES), 1)
    odd = column % 2 == 1
    upper_odd = (column >= 63) & (column < 127)
    packing = jnp.where(
        odd, jnp.where(upper_odd, 63, 127), jnp.where(column < ROWS, 0, ROWS)
    )
    edge_row = row % 2 == 1
    target = jnp.where(
        edge_row,
        jnp.where((row >= 63) & (row < 127), 0, ROWS),
        jnp.where(row < ROWS, 63, 127),
    )
    for place, chosen_lanes in enumerate(
        (
            (row == column + 1) & (column % ROWS != ROWS - 1),
            (row == column - 1) & (column % ROWS != 0),
            row == (column + ROWS) % LANES,
            row == packing,
        )
    ):
        shifts[:, place * LANES : (place + 1) * LANES] = jnp.where(chosen_lanes, 1.0, 0.0).astype(BF16)
    spread[...] = jnp.where(column == target, 1.0, 0.0).astype(BF16)

    position = lax.broadcasted_iota(jnp.int32, (16, 2 * LANES), 1)
    for t in range(PAIRS):
        choose[t] = jnp.where((((position + 1) & 63) >> 1) == t, 1.0, 0.0).astype(BF16)

    def parts(value):
        high = value.astype(BF16)
        rest = (value - high.astype(F32)).astype(BF16)
        return jnp.concatenate([high, rest], axis=1)

    stacked = LEVELS * SLOTS
    strip_copies = [None] * 4

    def shift_field(number):
        def shift_all(chunk, acc):
            first = chunk * CHUNK
            pieces = []
            for i in range(CHUNK):
                value = q[number, :, tile(first + i)]
                if number == 0:
                    value = value - q[1, :, tile(first + i)]
                    q[0, :, tile(first + i)] = value
                pieces.append(parts(value))
            split_parts = jnp.concatenate(pieces, axis=0)
            moved = jnp.dot(split_parts, shifts[...], preferred_element_type=F32)
            for i in range(CHUNK):
                rows = slice(i * stacked, (i + 1) * stacked)
                east_of[number, :, tile(first + i)] = moved[rows, :LANES]
                west_of[number, :, tile(first + i)] = moved[rows, LANES : 2 * LANES]
                half_of[number, :, tile(first + i + 1)] = moved[rows, 2 * LANES : 3 * LANES]
                here = (((lane_all + 1) & 63) >> 1) == first + i
                acc = jnp.where(here, moved[rows, 3 * LANES :], acc)
            return acc

        strips[number, 0] = lax.fori_loop(
            0, PAIRS // CHUNK, shift_all, jnp.zeros((stacked, LANES), F32)
        )
        for t in (0, PAIRS + 1):
            half_of[number, :, tile(t)] = jnp.zeros((stacked, LANES), F32)
        strips[number, 1] = jnp.where(
            lane_all < ROWS, q[number, :, tile(0)], q[number, :, tile(PAIRS - 1)]
        )
        strip_copies[number] = send_strips(number)

    loads[0].wait()
    loads[1].wait()
    pl.semaphore_wait(barrier, len(partners))
    shift_field(0)

    flag_load.wait()
    weight = jnp.zeros((SLOTS, LANES), F32)
    for b in range(SLOTS):
        flag = jnp.where(flags[pos * SLOTS + b] > 0, 1.0, 0.0)
        weight = jnp.where(slot == b, flag, weight)

    loads[4].wait()
    loads[5].wait()

    def wide_strips(value_of, store):
        for group in range(4):
            packed = jnp.zeros((SLOTS, LANES), F32)
            for k in range(8):
                value = value_of[8 * group + k]
                moved = pltpu.roll(value, 8 * k, 1) if k else value
                packed = jnp.where((((lane + 4) & 63) >> 3) == k, moved, packed)
            store[group] = packed
        for place, t in enumerate((0, 1, PAIRS - 2, PAIRS - 1)):
            store[4 + place] = value_of[t]

    def diagonal(t, _):
        centre = 6.0 + cc[:, tile(t)]
        mi2[t] = weight / centre
        mrow[2 * t] = jnp.where(low_half, centre, 0.0)
        mrow[2 * t + 1] = jnp.where(low_half, pltpu.roll(centre, 64, 1), 0.0)
        return 0

    lax.fori_loop(0, PAIRS, diagonal, 0, unroll=8)
    wide_strips(mi2, mstrips)

    def exchange(store, landing, send_sem, recv_sem):
        copies = []
        for side in range(2):
            copy = pltpu.make_async_remote_copy(
                src_ref=store,
                dst_ref=landing.at[1 - side],
                send_sem=send_sem.at[side],
                recv_sem=recv_sem.at[1 - side],
                device_id=ring[side],
                device_id_type=MESH,
            )
            copy.start()
            copies.append(copy)
        return copies

    m_copies = exchange(mstrips, marrived, m_send, m_recv)

    listed_lanes = pltpu.roll(
        own_lists[...].astype(F32), (LANES - (pos % (LANES // SLOTS)) * SLOTS) % LANES, 1
    )
    chosen = []
    for direction in range(8):
        line = jnp.broadcast_to(listed_lanes[direction : direction + 1], (SLOTS, LANES))
        own = jnp.sum(jnp.where(lane == slot, line, 0.0), axis=1, keepdims=True)
        listed = jnp.broadcast_to(own, (SLOTS, LANES)).astype(jnp.int32)
        column = (listed - (pos - 1) * SLOTS + total * SLOTS) % (total * SLOTS)
        there = listed >= 0
        which = column // SLOTS
        row = jnp.where(there, column % SLOTS, 0)
        chosen.append((row, [there & (which == side) for side in range(3)]))

    def take(direction, sources):
        row, sides = chosen[direction]
        result = jnp.zeros((SLOTS, LANES), F32)
        for source, side in zip(sources, sides):
            result = jnp.where(side, jnp.take_along_axis(source, row, axis=0), result)
        return result

    east_edge = (lane & 63) == 63
    west_edge = (lane & 63) == 0

    def inside(numbers, t):
        total_gap = jnp.zeros((SLOTS, LANES), F32)
        for level in range(LEVELS):
            rows = pl.ds(level * SLOTS, SLOTS)
            zonal = q[2, rows, tile(t)]
            meridional = q[3, rows, tile(t)]
            from_west = zonal > 0.0
            from_south = meridional > 0.0
            behind = low_half & from_south
            beyond = jnp.logical_not(low_half | from_south)
            speed_x = jnp.abs(zonal)
            speed_y = jnp.abs(meridional)
            stay = 1.0 - speed_x - speed_y
            if 0 in numbers:
                outside = (east_edge & jnp.logical_not(from_west)) | (west_edge & from_west)
                inward[rows, tile(t)] = jnp.where(outside, speed_x, 0.0)
            for number in numbers:
                along = jnp.where(from_west, west_of[number, rows, tile(t)], east_of[number, rows, tile(t)])
                across = jnp.where(beyond, half_of[number, rows, tile(t + 2)], half_of[number, rows, tile(t + 1)])
                across = jnp.where(behind, half_of[number, rows, tile(t)], across)
                moved = stay * q[number, rows, tile(t)] + speed_x * along + speed_y * across
                east_of[number, rows, tile(t)] = moved
                if number == 0:
                    total_gap = total_gap + moved
        return total_gap

    for i in (2, 3, 7):
        loads[i].wait()

    def first_load(t, _):
        z2[t] = src[:, tile(t)] + inside((0,), t) * (1.0 / LEVELS)
        return 0

    lax.fori_loop(0, PAIRS, first_load, 0)

    def share(use, group, value):
        phase = 2 * use + group
        peers, own = groups[group]
        store, landing = part.at[phase], (near_sums, far_sums)[group].at[use]
        store[0:1] = value
        landing[pl.ds(own, 1)] = value
        for peer in peers:
            pltpu.make_async_remote_copy(
                src_ref=store.at[pl.ds(0, 1)],
                dst_ref=landing.at[pl.ds(own, 1)],
                send_sem=sum_send.at[phase],
                recv_sem=sum_recv.at[phase],
                device_id=peer,
                device_id_type=MESH,
            ).start()

    def gather_sum(use, group):
        phase = 2 * use + group
        peers, _ = groups[group]
        landing = (near_sums, far_sums)[group].at[use]
        every = landing.at[pl.ds(0, len(peers))]
        copies = pltpu.make_async_remote_copy(
            src_ref=every,
            dst_ref=every,
            send_sem=sum_send.at[phase],
            recv_sem=sum_recv.at[phase],
            device_id=ring[0],
            device_id_type=MESH,
        )
        copies.wait_recv()
        copies.wait_send()
        return jnp.sum(landing[...], axis=0, keepdims=True)

    def spread_out(sums):
        return [jnp.broadcast_to(sums[:, i : i + 1], (SLOTS, LANES)) for i in range(8)]

    def gathered(values):
        result = jnp.zeros((SLOTS, LANES), F32)
        for place, value in enumerate(values):
            result = jnp.where(slot == place, jnp.sum(value, axis=0, keepdims=True), result)
        column = jnp.sum(result, axis=1, keepdims=True)
        return jnp.sum(jnp.where(lane == slot, column, 0.0), axis=0, keepdims=True)

    zero = jnp.zeros((SLOTS, LANES), F32)

    def split(t, carry):
        last, line, norm, product = carry
        value = z2[t] * mi2[t]
        for row, moved in ((2 * t, value), (2 * t + 1, pltpu.roll(value, 64, 1))):
            here = jnp.where(low_half, moved, 0.0)
            ahead = pltpu.roll(here, LANES - 1, 1)
            wide = here + 0.5 * (ahead + pltpu.roll(here, 1, 1))
            norm = norm + here * here * mrow[row]
            product = product + (here * ahead + last * wide)
            last = here
        return last, line, norm, product

    _, _, norm, product = lax.fori_loop(0, PAIRS, split, (zero, zero, zero, zero), unroll=8)
    share(0, 0, gathered([norm, 2.0 * product]))

    for number in (1, 2, 3):
        shift_field(number)
    share(0, 1, gather_sum(0, 0))

    def fill_halos(number):
        for copy in strip_copies[number]:
            copy.wait()

        for level in range(LEVELS):
            rows = pl.ds(level * SLOTS, SLOTS)
            sides = [arrived[0, number, 0, rows], strips[number, 0, rows], arrived[1, number, 0, rows]]
            hx[number, rows] = jnp.where((lane & 1) == 1, take(1, sides), take(0, sides))
            ends = [arrived[0, number, 1, rows], strips[number, 1, rows], arrived[1, number, 1, rows]]
            end = jnp.where(low_half, take(2, ends), take(3, ends))
            end = pltpu.roll(end, 64, 1)
            first = q[3, rows, tile(0)]
            last = q[3, rows, tile(PAIRS - 1)]
            below = jnp.where(low_half & (first > 0.0), first, 0.0) * end
            above = jnp.where(low_half | (last > 0.0), 0.0, -last) * end
            east_of[number, rows, tile(0)] += below
            east_of[number, rows, tile(PAIRS - 1)] += above
            if number == 0:
                z2[0] += below * (1.0 / LEVELS)
                z2[PAIRS - 1] += above * (1.0 / LEVELS)
        halo_parts = parts(hx[number])

        for chunk in range(PAIRS // CHUNK):
            first = chunk * CHUNK
            pieces = []
            for i in range(CHUNK):
                pieces += [halo_parts[16 * j : 16 * j + 16] * choose[first + i] for j in range(4)]
            found = jnp.dot(
                jnp.concatenate(pieces, axis=0), spread[...], preferred_element_type=F32
            )
            for i in range(CHUNK):
                edge_of[number, :, tile(first + i)] = found[i * stacked : (i + 1) * stacked]

    def advance(numbers, t):
        carried = {number: [] for number in numbers}
        for level in range(LEVELS):
            rows = pl.ds(level * SLOTS, SLOTS)
            inverse = ip[rows, tile(t)]
            entering = inward[rows, tile(t)]
            for number in numbers:
                moved = east_of[number, rows, tile(t)] + entering * edge_of[number, rows, tile(t)]
                value = moved * inverse
                if level > 0:
                    value = value + gl[rows, tile(t)] * carried[number][-1]
                carried[number].append(value)
        solved = {}
        for number in numbers:
            values = carried[number]
            for level in range(LEVELS - 2, -1, -1):
                rows = pl.ds(level * SLOTS, SLOTS)
                values[level] = values[level] + fu[rows, tile(t)] * values[level + 1]
            solved[number] = values
        for number in numbers:
            for level in range(LEVELS):
                value = solved[number][level]
                if number == 0:
                    value = value + solved[1][level]
                mixed[number, pl.ds(level * SLOTS, SLOTS), tile(t)] = value

    outs = (t_out, s_out, u_out, v_out)

    def write_out(number):
        copy = pltpu.make_async_copy(mixed.at[number], outs[number], out_sem.at[number])
        copy.start()
        return copy

    fill_halos(0)

    def whole_load(t, _):
        entering = jnp.zeros((SLOTS, LANES), F32)
        for level in range(LEVELS):
            rows = pl.ds(level * SLOTS, SLOTS)
            entering = entering + inward[rows, tile(t)] * edge_of[0, rows, tile(t)]
        z2[t] = (z2[t] + entering * (1.0 / LEVELS)) * mi2[t]
        return 0

    lax.fori_loop(0, PAIRS, whole_load, 0, unroll=4)
    wide_strips(z2, zstrips)
    z_copies = exchange(zstrips, zarrived, z_send, z_recv)

    def others_inside(t, _):
        inside((1, 2, 3), t)
        return 0

    lax.fori_loop(0, PAIRS, others_inside, 0)
    loads[6].wait()

    def factor(t, _):
        above = None
        for level in range(LEVELS):
            rows = pl.ds(level * SLOTS, SLOTS)
            pivot = 1.0
            if level > 0:
                lower = kk[pl.ds((level - 1) * SLOTS, SLOTS), tile(t)]
                pivot = pivot + lower
            if level < LEVELS - 1:
                upper = kk[rows, tile(t)]
                pivot = pivot + upper
            if level > 0:
                pivot = pivot - lower * above
            inverse = 1.0 / pivot
            ip[rows, tile(t)] = inverse * weight
            if level > 0:
                gl[rows, tile(t)] = lower * inverse
            if level < LEVELS - 1:
                above = upper * inverse
                fu[rows, tile(t)] = above
        return 0

    lax.fori_loop(0, PAIRS, factor, 0, unroll=2)


    def widen(store, landing, halves, wide, interior):
        def sources(place):
            return [landing[0, place], store[place], landing[1, place]]

        for first, directions, places in (
            (0, (3, 6, 7), (6, 7)),
            (HALO + ROWS, (2, 4, 5), (4, 5)),
        ):
            for i, place in enumerate(places):
                line = take(directions[0], sources(place))
                corner = jnp.where(
                    (lane & 63) < 32,
                    take(directions[1], sources(place)),
                    take(directions[2], sources(place)),
                )
                wide[first + 2 * i] = jnp.where(low_half, line, pltpu.roll(corner, 64, 1))
                wide[first + 2 * i + 1] = jnp.where(low_half, pltpu.roll(line, 64, 1), corner)
        for group in range(4):
            halves[group] = jnp.where(
                (lane & 4) == 0, take(0, sources(group)), take(1, sources(group))
            )

        def rows(t, _):
            side = halves[t // 8]
            step = (8 * t) % ROWS
            even, odd = interior(t)
            wide[HALO + 2 * t] = jnp.where(low_half, even, pltpu.roll(side, 64 - step, 1))
            wide[HALO + 2 * t + 1] = jnp.where(
                low_half, odd, pltpu.roll(side, (LANES - step) % LANES, 1)
            )
            return 0

        lax.fori_loop(0, PAIRS, rows, 0, unroll=8)

    for copy in m_copies:
        copy.wait()
    widen(mstrips, marrived, v1, mx, lambda t: (mi2[t], pltpu.roll(mi2[t], 64, 1)))
    for copy in z_copies:
        copy.wait()
    widen(
        zstrips, zarrived, v1, zx,
        lambda t: (z2[t], pltpu.roll(z2[t], 64, 1)),
    )

    def neighbours(value):
        paired = pltpu.roll(value, 1, 1) + pltpu.roll(value, LANES - 1, 1)
        return paired, value + 0.5 * paired

    basis = [zx, v1, v2, v3, v4]
    moments = []
    shift = None
    for power in range(4):
        old, new = basis[power], basis[power + 1]
        first, last = 1 + power, HALO + ROWS + 2 - power
        def read(a, power=power, old=old, shift=shift):
            value = old[a]
            if power:
                value = value - shift * basis[power - 1][a]
                old[a] = value
            return value

        def advance_row(a, carry, new=new, read=read):
            here, paired, wide, behind = carry
            ahead = read(a + 1)
            ahead_paired, ahead_wide = neighbours(ahead)
            value = mx[a] * (paired + behind + ahead_wide)
            new[a] = value
            return (ahead, ahead_paired, ahead_wide, wide), here, value

        behind = read(first - 1)
        here = read(first)
        carry = (here, *neighbours(here), neighbours(behind)[1])
        for a in range(first, HALO):
            carry, _, _ = advance_row(a, carry)

        def inner(r, state, power=power, advance_row=advance_row, shift=shift):
            carry, same, cross = state
            carry, here, value = advance_row(r + HALO, carry)
            weighed = mrow[r] * here
            if power == 0:
                return carry, same + here * weighed, cross
            if power == 3:
                value = value - shift * here
                return carry, same + here * weighed, (cross[0] + basis[2][r + HALO] * weighed, cross[1] + weighed * value)
            return carry, same + here * weighed, cross + basis[power - 1][r + HALO] * weighed

        start = (zero, zero) if power == 3 else zero
        carry, same, cross = lax.fori_loop(0, ROWS, inner, (carry, zero, start), unroll=16)
        if power:
            moments.append(cross[0] if power == 3 else cross)
        moments.append(same)
        if power == 3:
            moments.append(cross[1])
        for a in range(HALO + ROWS, last + 1):
            carry, _, _ = advance_row(a, carry)
        if power == 0:
            both = spread_out(gather_sum(0, 1))
            shift = both[1] / both[0]

    share(1, 0, gathered(moments))
    for number in (1, 2, 3):
        fill_halos(number)

    def tracers(t, _):
        advance((0, 1), t)
        return 0

    lax.fori_loop(0, PAIRS, tracers, 0)
    out_copies = [write_out(0), write_out(1)]
    share(1, 1, gather_sum(1, 0))

    def velocities(t, _):
        advance((2, 3), t)
        return 0

    lax.fori_loop(0, PAIRS, velocities, 0)
    out_copies += [write_out(2), write_out(3)]
    mu = spread_out(gather_sum(1, 1))

    rest = 1.0 - shift
    matrix = [[rest * mu[i + j] - mu[i + j + 1] for j in range(4)] for i in range(4)]
    lower = [[None] * 4 for _ in range(4)]
    pivots, inverses, ahead = [], [], []
    for j in range(4):
        pivot = matrix[j][j]
        for i in range(j):
            pivot = pivot - lower[j][i] * lower[j][i] * pivots[i]
        kept = pivot > 1e-6 * matrix[j][j]
        pivots.append(jnp.where(kept, pivot, 0.0) if j else pivot)
        inverses.append(jnp.where(kept, 1.0 / pivot, 0.0) if j else 1.0 / pivot)
        for i in range(j + 1, 4):
            entry = matrix[i][j]
            for m in range(j):
                entry = entry - lower[i][m] * lower[j][m] * pivots[m]
            lower[i][j] = entry * inverses[j]
        right = mu[j]
        for i in range(j):
            right = right - lower[j][i] * ahead[i]
        ahead.append(right)
    factors = [None] * 4
    for j in range(3, -1, -1):
        value = ahead[j] * inverses[j]
        for i in range(j + 1, 4):
            value = value - lower[i][j] * factors[i]
        factors[j] = value

    def level_row(a):
        value = factors[0] * basis[0][a]
        for j in range(1, 4):
            value = value + factors[j] * basis[j][a]
        return value

    def slopes(t, carry):
        behind, here = carry
        ahead = level_row(HALO + 2 * t + 1)
        beyond = level_row(HALO + 2 * t + 2)

        def zonal_slope(value):
            return 0.5 * (pltpu.roll(value, LANES - 1, 1) - pltpu.roll(value, 1, 1))

        def joined(even, odd):
            return jnp.where(low_half, even, pltpu.roll(odd, 64, 1))

        sx_out[:, tile(t)] = joined(zonal_slope(here), zonal_slope(ahead))
        sy_out[:, tile(t)] = joined(0.5 * (ahead - behind), 0.5 * (beyond - here))
        h_out[:, tile(t)] = joined(here, ahead)
        return ahead, beyond

    lax.fori_loop(0, PAIRS, slopes, (level_row(HALO - 1), level_row(HALO)), unroll=8)
    for copy in out_copies:
        copy.wait()


def finish_kernel(t_in, s_in, u_in, v_in, sx, sy, h, t_out, s_out, u_out, v_out, h_out, u, v, sems):
    copies = [
        pltpu.make_async_copy(source, target, sems.at[i])
        for i, (source, target) in enumerate(((t_in, t_out), (s_in, s_out), (h, h_out)))
    ]
    for copy in copies:
        copy.start()
    width = CELLS // PARTS
    for i in range(PARTS):
        columns = pl.ds(i * width, width)
        for n, (source, slope, store, target) in enumerate(
            ((u_in, sx, u, u_out), (v_in, sy, v, v_out))
        ):
            for level in range(LEVELS):
                rows = pl.ds(level * SLOTS, SLOTS)
                store[rows, columns] = source[rows, columns] - slope[:, columns]
            copy = pltpu.make_async_copy(
                store.at[:, columns], target.at[:, columns], sems.at[3 + 2 * i + n]
            )
            copy.start()
            copies.append(copy)
    for copy in copies:
        copy.wait()


def finish(fields, extras):
    vmem = pl.BlockSpec(memory_space=pltpu.VMEM)
    hbm = pl.BlockSpec(memory_space=pltpu.HBM)
    big = jax.ShapeDtypeStruct((LEVELS * SLOTS, CELLS), F32)
    small = jax.ShapeDtypeStruct((SLOTS, CELLS), F32)
    return pl.pallas_call(
        finish_kernel,
        in_specs=[vmem] * 7,
        out_specs=[hbm] * 5,
        out_shape=[big] * 4 + [small],
        scratch_shapes=[
            pltpu.VMEM((LEVELS * SLOTS, CELLS), F32),
            pltpu.VMEM((LEVELS * SLOTS, CELLS), F32),
            pltpu.SemaphoreType.DMA((3 + 2 * PARTS,)),
        ],
        compiler_params=pltpu.CompilerParams(vmem_limit_bytes=16 * 1024 * 1024),
        name="finish",
    )(*fields, *extras)


def local(sizes, t, s, u, v, k, c, g, flags, lists):
    stacked = LEVELS * SLOTS
    fields = [x.reshape(stacked, CELLS) for x in (t, s, u, v)]
    big = jax.ShapeDtypeStruct((stacked, CELLS), F32)
    small = jax.ShapeDtypeStruct((SLOTS, CELLS), F32)
    anywhere = pl.BlockSpec(memory_space=pl.ANY)
    held = pl.BlockSpec(memory_space=pltpu.HBM)
    vmem = pl.BlockSpec(memory_space=pltpu.VMEM)
    dma = pltpu.SemaphoreType.DMA
    total = sizes[0] * sizes[1]
    tall = ROWS + 2 * HALO
    results = pl.pallas_call(
        functools.partial(kernel, sizes),
        out_shape=[big] * 4 + [small] * 3,
        in_specs=[held] * 9,
        out_specs=[anywhere] * 4 + [vmem] * 3,
        scratch_shapes=[
            pltpu.VMEM((4, stacked, CELLS), F32),
            pltpu.VMEM((stacked - SLOTS, CELLS), F32),
            pltpu.VMEM((SLOTS, CELLS), F32),
            pltpu.VMEM((SLOTS, CELLS), F32),
            pltpu.VMEM((8, LANES), jnp.int32),
            pltpu.SMEM((SLOTS * total,), jnp.int32),
            pltpu.VMEM((4, stacked, CELLS), F32),
            pltpu.VMEM((stacked, CELLS), F32),
            pltpu.VMEM((stacked, CELLS), F32),
            pltpu.VMEM((stacked, CELLS), F32),
            pltpu.VMEM((4, stacked, LANES), F32),
            pltpu.VMEM((4, stacked, CELLS), F32),
            pltpu.VMEM((4, stacked, CELLS), F32),
            pltpu.VMEM((4, stacked, CELLS + 2 * LANES), F32),
            pltpu.VMEM((4, stacked, CELLS), F32),
            pltpu.VMEM((2 * LANES, 4 * LANES), BF16),
            pltpu.VMEM((2 * LANES, LANES), BF16),
            pltpu.VMEM((4, 2, stacked, LANES), F32),
            pltpu.VMEM((2, 4, 2, stacked, LANES), F32),
            pltpu.VMEM((8, SLOTS, LANES), F32),
            pltpu.VMEM((2, 8, SLOTS, LANES), F32),
            pltpu.VMEM((8, SLOTS, LANES), F32),
            pltpu.VMEM((2, 8, SLOTS, LANES), F32),
            pltpu.VMEM((PAIRS, SLOTS, LANES), F32),
            pltpu.VMEM((PAIRS, SLOTS, LANES), F32),
            pltpu.VMEM((tall, SLOTS, LANES), F32),
            pltpu.VMEM((tall, SLOTS, LANES), F32),
            pltpu.VMEM((ROWS, SLOTS, LANES), F32),
            pltpu.VMEM((tall, SLOTS, LANES), F32),
            pltpu.VMEM((tall, SLOTS, LANES), F32),
            pltpu.VMEM((tall, SLOTS, LANES), F32),
            pltpu.VMEM((tall, SLOTS, LANES), F32),
            pltpu.VMEM((stacked, CELLS), F32),
            pltpu.VMEM((PAIRS, 16, 2 * LANES), BF16),
            pltpu.VMEM((4, SLOTS, LANES), F32),
            pltpu.VMEM((2, 8, LANES), F32),
            pltpu.VMEM((2, 16, LANES), F32),
            dma((9,)),
            dma((4,)),
            dma((2, 4)),
            dma((2, 4)),
            dma((2,)),
            dma((2,)),
            dma((2,)),
            dma((2,)),
            dma((4,)),
            dma((4,)),
        ],
        compiler_params=pltpu.CompilerParams(
            collective_id=0, has_side_effects=True, vmem_limit_bytes=40 * 1024 * 1024
        ),
        name="ocean_step",
    )(
        *[
            pltpu.with_memory_space_constraint(x, pltpu.HBM)
            for x in (*fields, k.reshape(stacked - SLOTS, CELLS), c, g, flags, lists.T)
        ],
    )
    done = finish(results[:4], results[4:])
    shape = (LEVELS, SLOTS, CELLS)
    return tuple(x.reshape(shape) for x in done[:4]) + (done[4],)


def solution(mesh):
    whole = P(None, ("gx", "gy"), None)
    flat = P(("gx", "gy"), None)
    return jax.shard_map(
        functools.partial(local, (mesh.shape["gx"], mesh.shape["gy"])),
        mesh=mesh,
        in_specs=(whole, whole, whole, whole, whole, flat, flat, P(), P()),
        out_specs=(whole, whole, whole, whole, flat),
        check_vma=False,
    )
```

```python
import functools
import itertools

import jax
import jax.numpy as jnp
from jax import lax
from jax.experimental import pallas as pl
from jax.experimental.pallas import tpu as pltpu
from jax.sharding import PartitionSpec as P

MESH = pl.DeviceIdType.MESH
F32 = jnp.float32
BF16 = jnp.bfloat16
LANES = 128
SLOTS = 8
LEVELS = 8
PAIRS = 32
CELLS = 4096
ROWS = 64
HALO = 4
CHUNK = 8
PARTS = 4


def tile(t):
    return pl.ds(pl.multiple_of(t * LANES, LANES), LANES)


def kernel(
    sizes,
    t_in, s_in, u_in, v_in, k_in, c_in, g_in, flags_in, lists,
    t_out, s_out, u_out, v_out, sx_out, sy_out, h_out,
    q, kk, cc, src, own_lists, flags, mixed, ip, fu, gl, hx,
    east_of, west_of, half_of, edge_of, shifts, spread,
    strips, arrived, mstrips, marrived, zstrips, zarrived,
    z2, mi2, zx, mx, mrow, v1, v2, v3, v4, inward, choose, part, near_sums, far_sums,
    in_sem, out_sem, strip_send, strip_recv, m_send, m_recv, z_send, z_recv, sum_send, sum_recv,
):
    count_x, count_y = sizes
    total = count_x * count_y
    gx, gy = lax.axis_index("gx"), lax.axis_index("gy")
    pos = gx * count_y + gy
    before, after = (pos + total - 1) % total, (pos + 1) % total
    ring = [(before // count_y, before % count_y), (after // count_y, after % count_y)]

    ys = [(gx + n) % 4 for n in range(4)]
    zs = [(gy // 8 + n) % 4 * 8 for n in range(4)]
    xs = [(gy // 2 + n) % 4 * 2 for n in range(4)]
    cores = [(gy + n) % 2 for n in range(2)]

    def hops(step):
        return -sum(min(n, 4 - n) for n in step)

    near_steps = sorted(itertools.product((0, 2, 1, 3), range(2)), key=lambda step: hops(step[:1]))
    far_steps = sorted(itertools.product(range(4), range(4)), key=hops)
    near = [(gx, zs[0] + xs[x] + cores[c]) for x, c in near_steps if x or c]
    far = [(ys[y], zs[z] + xs[0] + cores[0]) for y, z in far_steps if y or z]
    groups = ((near, gy % 8), (far, gx * 4 + gy // 8))
    partners = ring + far + near

    barrier = pltpu.get_barrier_semaphore()

    loads = []
    for number, ref in enumerate((t_in, s_in, u_in, v_in)):
        loads.append(pltpu.make_async_copy(ref, q.at[number], in_sem.at[number]))
    loads.append(pltpu.make_async_copy(
            lists.at[:, tile(pos // (LANES // SLOTS))], own_lists, in_sem.at[4]
        ))
    loads.append(pltpu.make_async_copy(c_in, cc, in_sem.at[5]))
    loads.append(pltpu.make_async_copy(k_in, kk, in_sem.at[6]))
    loads.append(pltpu.make_async_copy(g_in, src, in_sem.at[7]))
    for load in loads[:2]:
        load.start()
    for other in partners:
        pl.semaphore_signal(barrier, inc=1, device_id=other, device_id_type=MESH)
    for load in loads[2:]:
        load.start()
    flag_load = pltpu.make_async_copy(flags_in, flags, in_sem.at[8])
    flag_load.start()

    lane = lax.broadcasted_iota(jnp.int32, (SLOTS, LANES), 1)
    slot = lax.broadcasted_iota(jnp.int32, (SLOTS, LANES), 0)
    low_half = lane < ROWS
    lane_all = lax.broadcasted_iota(jnp.int32, (LEVELS * SLOTS, LANES), 1)

    def send_strips(number):
        copies = []
        for side in range(2):
            copy = pltpu.make_async_remote_copy(
                src_ref=strips.at[number],
                dst_ref=arrived.at[1 - side, number],
                send_sem=strip_send.at[side, number],
                recv_sem=strip_recv.at[1 - side, number],
                device_id=ring[side],
                device_id_type=MESH,
            )
            copy.start()
            copies.append(copy)
        return copies

    row = lax.broadcasted_iota(jnp.int32, (2 * LANES, LANES), 0) % LANES
    column = lax.broadcasted_iota(jnp.int32, (2 * LANES, LANES), 1)
    odd = column % 2 == 1
    upper_odd = (column >= 63) & (column < 127)
    packing = jnp.where(
        odd, jnp.where(upper_odd, 63, 127), jnp.where(column < ROWS, 0, ROWS)
    )
    edge_row = row % 2 == 1
    target = jnp.where(
        edge_row,
        jnp.where((row >= 63) & (row < 127), 0, ROWS),
        jnp.where(row < ROWS, 63, 127),
    )
    for place, chosen_lanes in enumerate(
        (
            (row == column + 1) & (column % ROWS != ROWS - 1),
            (row == column - 1) & (column % ROWS != 0),
            row == (column + ROWS) % LANES,
            row == packing,
        )
    ):
        shifts[:, place * LANES : (place + 1) * LANES] = jnp.where(chosen_lanes, 1.0, 0.0).astype(BF16)
    spread[...] = jnp.where(column == target, 1.0, 0.0).astype(BF16)

    position = lax.broadcasted_iota(jnp.int32, (16, 2 * LANES), 1)
    for t in range(PAIRS):
        choose[t] = jnp.where((((position + 1) & 63) >> 1) == t, 1.0, 0.0).astype(BF16)

    def parts(value):
        high = value.astype(BF16)
        rest = (value - high.astype(F32)).astype(BF16)
        return jnp.concatenate([high, rest], axis=1)

    stacked = LEVELS * SLOTS
    strip_copies = [None] * 4

    def shift_field(number):
        def shift_all(chunk, acc):
            first = chunk * CHUNK
            pieces = []
            for i in range(CHUNK):
                value = q[number, :, tile(first + i)]
                if number == 0:
                    value = value - q[1, :, tile(first + i)]
                    q[0, :, tile(first + i)] = value
                pieces.append(parts(value))
            split_parts = jnp.concatenate(pieces, axis=0)
            moved = jnp.dot(split_parts, shifts[...], preferred_element_type=F32)
            for i in range(CHUNK):
                rows = slice(i * stacked, (i + 1) * stacked)
                east_of[number, :, tile(first + i)] = moved[rows, :LANES]
                west_of[number, :, tile(first + i)] = moved[rows, LANES : 2 * LANES]
                half_of[number, :, tile(first + i + 1)] = moved[rows, 2 * LANES : 3 * LANES]
                here = (((lane_all + 1) & 63) >> 1) == first + i
                acc = jnp.where(here, moved[rows, 3 * LANES :], acc)
            return acc

        strips[number, 0] = lax.fori_loop(
            0, PAIRS // CHUNK, shift_all, jnp.zeros((stacked, LANES), F32), unroll=2
        )
        for t in (0, PAIRS + 1):
            half_of[number, :, tile(t)] = jnp.zeros((stacked, LANES), F32)
        strips[number, 1] = jnp.where(
            lane_all < ROWS, q[number, :, tile(0)], q[number, :, tile(PAIRS - 1)]
        )

    loads[0].wait()
    loads[1].wait()
    shift_field(0)
    pl.semaphore_wait(barrier, len(partners))
    strip_copies[0] = send_strips(0)

    flag_load.wait()
    weight = jnp.zeros((SLOTS, LANES), F32)
    for b in range(SLOTS):
        flag = jnp.where(flags[pos * SLOTS + b] > 0, 1.0, 0.0)
        weight = jnp.where(slot == b, flag, weight)

    loads[4].wait()
    loads[5].wait()

    def wide_strips(value_of, store):
        for group in range(4):
            packed = jnp.zeros((SLOTS, LANES), F32)
            for k in range(8):
                value = value_of[8 * group + k]
                moved = pltpu.roll(value, 8 * k, 1) if k else value
                packed = jnp.where((((lane + 4) & 63) >> 3) == k, moved, packed)
            store[group] = packed
        for place, t in enumerate((0, 1, PAIRS - 2, PAIRS - 1)):
            store[4 + place] = value_of[t]

    def diagonal(t, _):
        centre = 6.0 + cc[:, tile(t)]
        mi2[t] = weight / centre
        mrow[2 * t] = jnp.where(low_half, centre, 0.0)
        mrow[2 * t + 1] = jnp.where(low_half, pltpu.roll(centre, 64, 1), 0.0)
        return 0

    lax.fori_loop(0, PAIRS, diagonal, 0, unroll=8)
    wide_strips(mi2, mstrips)

    def exchange(store, landing, send_sem, recv_sem):
        copies = []
        for side in range(2):
            copy = pltpu.make_async_remote_copy(
                src_ref=store,
                dst_ref=landing.at[1 - side],
                send_sem=send_sem.at[side],
                recv_sem=recv_sem.at[1 - side],
                device_id=ring[side],
                device_id_type=MESH,
            )
            copy.start()
            copies.append(copy)
        return copies

    m_copies = exchange(mstrips, marrived, m_send, m_recv)

    listed_lanes = pltpu.roll(
        own_lists[...].astype(F32), (LANES - (pos % (LANES // SLOTS)) * SLOTS) % LANES, 1
    )
    chosen = []
    for direction in range(8):
        line = jnp.broadcast_to(listed_lanes[direction : direction + 1], (SLOTS, LANES))
        own = jnp.sum(jnp.where(lane == slot, line, 0.0), axis=1, keepdims=True)
        listed = jnp.broadcast_to(own, (SLOTS, LANES)).astype(jnp.int32)
        column = (listed - (pos - 1) * SLOTS + total * SLOTS) % (total * SLOTS)
        there = listed >= 0
        which = column // SLOTS
        row = jnp.where(there, column % SLOTS, 0)
        chosen.append((row, [there & (which == side) for side in range(3)]))

    def take(direction, sources):
        row, sides = chosen[direction]
        result = jnp.zeros((SLOTS, LANES), F32)
        for source, side in zip(sources, sides):
            result = jnp.where(side, jnp.take_along_axis(source, row, axis=0), result)
        return result

    east_edge = (lane & 63) == 63
    west_edge = (lane & 63) == 0

    def inside(numbers, t):
        total_gap = jnp.zeros((SLOTS, LANES), F32)
        for level in range(LEVELS):
            rows = pl.ds(level * SLOTS, SLOTS)
            zonal = q[2, rows, tile(t)]
            meridional = q[3, rows, tile(t)]
            from_west = zonal > 0.0
            from_south = meridional > 0.0
            behind = low_half & from_south
            beyond = jnp.logical_not(low_half | from_south)
            speed_x = jnp.abs(zonal)
            speed_y = jnp.abs(meridional)
            stay = 1.0 - speed_x - speed_y
            if 0 in numbers:
                outside = (east_edge & jnp.logical_not(from_west)) | (west_edge & from_west)
                inward[rows, tile(t)] = jnp.where(outside, speed_x, 0.0)
            for number in numbers:
                along = jnp.where(from_west, west_of[number, rows, tile(t)], east_of[number, rows, tile(t)])
                across = jnp.where(beyond, half_of[number, rows, tile(t + 2)], half_of[number, rows, tile(t + 1)])
                across = jnp.where(behind, half_of[number, rows, tile(t)], across)
                moved = stay * q[number, rows, tile(t)] + speed_x * along + speed_y * across
                east_of[number, rows, tile(t)] = moved
                if number == 0:
                    total_gap = total_gap + moved
        return total_gap

    for i in (2, 3, 7):
        loads[i].wait()

    def first_load(t, _):
        z2[t] = src[:, tile(t)] + inside((0,), t) * (1.0 / LEVELS)
        return 0

    lax.fori_loop(0, PAIRS, first_load, 0)

    def share(use, group, value):
        phase = 2 * use + group
        peers, own = groups[group]
        store, landing = part.at[phase], (near_sums, far_sums)[group].at[use]
        store[0:1] = value
        landing[pl.ds(own, 1)] = value
        for peer in peers:
            pltpu.make_async_remote_copy(
                src_ref=store.at[pl.ds(0, 1)],
                dst_ref=landing.at[pl.ds(own, 1)],
                send_sem=sum_send.at[phase],
                recv_sem=sum_recv.at[phase],
                device_id=peer,
                device_id_type=MESH,
            ).start()

    def gather_sum(use, group):
        phase = 2 * use + group
        peers, _ = groups[group]
        landing = (near_sums, far_sums)[group].at[use]
        every = landing.at[pl.ds(0, len(peers))]
        copies = pltpu.make_async_remote_copy(
            src_ref=every,
            dst_ref=every,
            send_sem=sum_send.at[phase],
            recv_sem=sum_recv.at[phase],
            device_id=ring[0],
            device_id_type=MESH,
        )
        copies.wait_recv()
        copies.wait_send()
        return jnp.sum(landing[...], axis=0, keepdims=True)

    def spread_out(sums):
        return [jnp.broadcast_to(sums[:, i : i + 1], (SLOTS, LANES)) for i in range(8)]

    def gathered(values):
        result = jnp.zeros((SLOTS, LANES), F32)
        for place, value in enumerate(values):
            result = jnp.where(slot == place, jnp.sum(value, axis=0, keepdims=True), result)
        column = jnp.sum(result, axis=1, keepdims=True)
        return jnp.sum(jnp.where(lane == slot, column, 0.0), axis=0, keepdims=True)

    zero = jnp.zeros((SLOTS, LANES), F32)

    def split(t, carry):
        last, line, norm, product = carry
        value = z2[t] * mi2[t]
        for row, moved in ((2 * t, value), (2 * t + 1, pltpu.roll(value, 64, 1))):
            here = jnp.where(low_half, moved, 0.0)
            ahead = pltpu.roll(here, LANES - 1, 1)
            wide = here + 0.5 * (ahead + pltpu.roll(here, 1, 1))
            norm = norm + here * here * mrow[row]
            product = product + (here * ahead + last * wide)
            last = here
        return last, line, norm, product

    _, _, norm, product = lax.fori_loop(0, PAIRS, split, (zero, zero, zero, zero), unroll=8)
    share(0, 0, gathered([norm, 2.0 * product]))

    for number in (1, 2, 3):
        shift_field(number)

    def fill_halos(number):
        for copy in strip_copies[number]:
            copy.wait()

        for level in range(LEVELS):
            rows = pl.ds(level * SLOTS, SLOTS)
            sides = [arrived[0, number, 0, rows], strips[number, 0, rows], arrived[1, number, 0, rows]]
            hx[number, rows] = jnp.where((lane & 1) == 1, take(1, sides), take(0, sides))
            ends = [arrived[0, number, 1, rows], strips[number, 1, rows], arrived[1, number, 1, rows]]
            end = jnp.where(low_half, take(2, ends), take(3, ends))
            end = pltpu.roll(end, 64, 1)
            first = q[3, rows, tile(0)]
            last = q[3, rows, tile(PAIRS - 1)]
            below = jnp.where(low_half & (first > 0.0), first, 0.0) * end
            above = jnp.where(low_half | (last > 0.0), 0.0, -last) * end
            east_of[number, rows, tile(0)] += below
            east_of[number, rows, tile(PAIRS - 1)] += above
            if number == 0:
                z2[0] += below * (1.0 / LEVELS)
                z2[PAIRS - 1] += above * (1.0 / LEVELS)
        halo_parts = parts(hx[number])

        for chunk in range(PAIRS // CHUNK):
            first = chunk * CHUNK
            pieces = []
            for i in range(CHUNK):
                pieces += [halo_parts[16 * j : 16 * j + 16] * choose[first + i] for j in range(4)]
            found = jnp.dot(
                jnp.concatenate(pieces, axis=0), spread[...], preferred_element_type=F32
            )
            for i in range(CHUNK):
                edge_of[number, :, tile(first + i)] = found[i * stacked : (i + 1) * stacked]

    def advance(numbers, t):
        carried = {number: [] for number in numbers}
        for level in range(LEVELS):
            rows = pl.ds(level * SLOTS, SLOTS)
            inverse = ip[rows, tile(t)]
            entering = inward[rows, tile(t)]
            for number in numbers:
                moved = east_of[number, rows, tile(t)] + entering * edge_of[number, rows, tile(t)]
                value = moved * inverse
                if level > 0:
                    value = value + gl[rows, tile(t)] * carried[number][-1]
                carried[number].append(value)
        solved = {}
        for number in numbers:
            values = carried[number]
            for level in range(LEVELS - 2, -1, -1):
                rows = pl.ds(level * SLOTS, SLOTS)
                values[level] = values[level] + fu[rows, tile(t)] * values[level + 1]
            solved[number] = values
        for number in numbers:
            for level in range(LEVELS):
                value = solved[number][level]
                if number == 0:
                    value = value + solved[1][level]
                mixed[number, pl.ds(level * SLOTS, SLOTS), tile(t)] = value

    outs = (t_out, s_out, u_out, v_out)

    def write_out(number):
        copy = pltpu.make_async_copy(mixed.at[number], outs[number], out_sem.at[number])
        copy.start()
        return copy

    fill_halos(0)

    def whole_load(t, _):
        entering = jnp.zeros((SLOTS, LANES), F32)
        for level in range(LEVELS):
            rows = pl.ds(level * SLOTS, SLOTS)
            entering = entering + inward[rows, tile(t)] * edge_of[0, rows, tile(t)]
        z2[t] = (z2[t] + entering * (1.0 / LEVELS)) * mi2[t]
        return 0

    lax.fori_loop(0, PAIRS, whole_load, 0, unroll=8)
    wide_strips(z2, zstrips)
    z_copies = exchange(zstrips, zarrived, z_send, z_recv)
    for number in (1, 2, 3):
        strip_copies[number] = send_strips(number)
    share(0, 1, gather_sum(0, 0))

    def others_inside(t, _):
        inside((1, 2, 3), t)
        return 0

    lax.fori_loop(0, PAIRS, others_inside, 0)
    loads[6].wait()

    def factor(t, _):
        above = None
        for level in range(LEVELS):
            rows = pl.ds(level * SLOTS, SLOTS)
            pivot = 1.0
            if level > 0:
                lower = kk[pl.ds((level - 1) * SLOTS, SLOTS), tile(t)]
                pivot = pivot + lower
            if level < LEVELS - 1:
                upper = kk[rows, tile(t)]
                pivot = pivot + upper
            if level > 0:
                pivot = pivot - lower * above
            inverse = 1.0 / pivot
            ip[rows, tile(t)] = inverse * weight
            if level > 0:
                gl[rows, tile(t)] = lower * inverse
            if level < LEVELS - 1:
                above = upper * inverse
                fu[rows, tile(t)] = above
        return 0

    lax.fori_loop(0, PAIRS, factor, 0, unroll=2)


    def widen(store, landing, halves, wide, interior):
        def sources(place):
            return [landing[0, place], store[place], landing[1, place]]

        for first, directions, places in (
            (0, (3, 6, 7), (6, 7)),
            (HALO + ROWS, (2, 4, 5), (4, 5)),
        ):
            for i, place in enumerate(places):
                line = take(directions[0], sources(place))
                corner = jnp.where(
                    (lane & 63) < 32,
                    take(directions[1], sources(place)),
                    take(directions[2], sources(place)),
                )
                wide[first + 2 * i] = jnp.where(low_half, line, pltpu.roll(corner, 64, 1))
                wide[first + 2 * i + 1] = jnp.where(low_half, pltpu.roll(line, 64, 1), corner)
        for group in range(4):
            halves[group] = jnp.where(
                (lane & 4) == 0, take(0, sources(group)), take(1, sources(group))
            )

        def rows(t, _):
            side = halves[t // 8]
            step = (8 * t) % ROWS
            even, odd = interior(t)
            wide[HALO + 2 * t] = jnp.where(low_half, even, pltpu.roll(side, 64 - step, 1))
            wide[HALO + 2 * t + 1] = jnp.where(
                low_half, odd, pltpu.roll(side, (LANES - step) % LANES, 1)
            )
            return 0

        lax.fori_loop(0, PAIRS, rows, 0, unroll=32)

    for copy in m_copies:
        copy.wait()
    widen(mstrips, marrived, v1, mx, lambda t: (mi2[t], pltpu.roll(mi2[t], 64, 1)))
    for copy in z_copies:
        copy.wait()
    widen(
        zstrips, zarrived, v1, zx,
        lambda t: (z2[t], pltpu.roll(z2[t], 64, 1)),
    )

    def neighbours(value):
        paired = pltpu.roll(value, 1, 1) + pltpu.roll(value, LANES - 1, 1)
        return paired, value + 0.5 * paired

    basis = [zx, v1, v2, v3, v4]
    moments = []
    shift = None
    for power in range(4):
        old, new = basis[power], basis[power + 1]
        first, last = 1 + power, HALO + ROWS + 2 - power
        def read(a, power=power, old=old, shift=shift):
            value = old[a]
            if power:
                value = value - shift * basis[power - 1][a]
                old[a] = value
            return value

        def advance_row(a, carry, new=new, read=read):
            here, paired, wide, behind = carry
            ahead = read(a + 1)
            ahead_paired, ahead_wide = neighbours(ahead)
            value = mx[a] * (paired + behind + ahead_wide)
            new[a] = value
            return (ahead, ahead_paired, ahead_wide, wide), here, value

        behind = read(first - 1)
        here = read(first)
        carry = (here, *neighbours(here), neighbours(behind)[1])
        for a in range(first, HALO):
            carry, _, _ = advance_row(a, carry)

        def inner(r, state, power=power, advance_row=advance_row, shift=shift):
            carry, same, cross = state
            carry, here, value = advance_row(r + HALO, carry)
            weighed = mrow[r] * here
            if power == 0:
                return carry, same + here * weighed, cross
            if power == 3:
                value = value - shift * here
                return carry, same + here * weighed, (cross[0] + basis[2][r + HALO] * weighed, cross[1] + weighed * value)
            return carry, same + here * weighed, cross + basis[power - 1][r + HALO] * weighed

        start = (zero, zero) if power == 3 else zero
        carry, same, cross = lax.fori_loop(0, ROWS, inner, (carry, zero, start), unroll=64)
        if power:
            moments.append(cross[0] if power == 3 else cross)
        moments.append(same)
        if power == 3:
            moments.append(cross[1])
        for a in range(HALO + ROWS, last + 1):
            carry, _, _ = advance_row(a, carry)
        if power == 0:
            both = spread_out(gather_sum(0, 1))
            shift = both[1] / both[0]

    share(1, 0, gathered(moments))
    for number in (1, 2, 3):
        fill_halos(number)

    def tracers(t, _):
        advance((0, 1), t)
        return 0

    lax.fori_loop(0, PAIRS, tracers, 0)
    out_copies = [write_out(0), write_out(1)]
    share(1, 1, gather_sum(1, 0))

    def velocities(t, _):
        advance((2, 3), t)
        return 0

    lax.fori_loop(0, PAIRS, velocities, 0)
    out_copies += [write_out(2), write_out(3)]
    mu = spread_out(gather_sum(1, 1))

    rest = 1.0 - shift
    matrix = [[rest * mu[i + j] - mu[i + j + 1] for j in range(4)] for i in range(4)]
    lower = [[None] * 4 for _ in range(4)]
    pivots, inverses, ahead = [], [], []
    for j in range(4):
        pivot = matrix[j][j]
        for i in range(j):
            pivot = pivot - lower[j][i] * lower[j][i] * pivots[i]
        kept = pivot > 1e-6 * matrix[j][j]
        pivots.append(jnp.where(kept, pivot, 0.0) if j else pivot)
        inverses.append(jnp.where(kept, 1.0 / pivot, 0.0) if j else 1.0 / pivot)
        for i in range(j + 1, 4):
            entry = matrix[i][j]
            for m in range(j):
                entry = entry - lower[i][m] * lower[j][m] * pivots[m]
            lower[i][j] = entry * inverses[j]
        right = mu[j]
        for i in range(j):
            right = right - lower[j][i] * ahead[i]
        ahead.append(right)
    factors = [None] * 4
    for j in range(3, -1, -1):
        value = ahead[j] * inverses[j]
        for i in range(j + 1, 4):
            value = value - lower[i][j] * factors[i]
        factors[j] = value

    def level_row(a):
        value = factors[0] * basis[0][a]
        for j in range(1, 4):
            value = value + factors[j] * basis[j][a]
        return value

    def slopes(t, carry):
        behind, here = carry
        ahead = level_row(HALO + 2 * t + 1)
        beyond = level_row(HALO + 2 * t + 2)

        def zonal_slope(value):
            return 0.5 * (pltpu.roll(value, LANES - 1, 1) - pltpu.roll(value, 1, 1))

        def joined(even, odd):
            return jnp.where(low_half, even, pltpu.roll(odd, 64, 1))

        sx_out[:, tile(t)] = joined(zonal_slope(here), zonal_slope(ahead))
        sy_out[:, tile(t)] = joined(0.5 * (ahead - behind), 0.5 * (beyond - here))
        h_out[:, tile(t)] = joined(here, ahead)
        return ahead, beyond

    lax.fori_loop(0, PAIRS, slopes, (level_row(HALO - 1), level_row(HALO)), unroll=32)
    for copy in out_copies:
        copy.wait()


def finish_kernel(t_in, s_in, u_in, v_in, sx, sy, h, t_out, s_out, u_out, v_out, h_out, u, v, sems):
    copies = [
        pltpu.make_async_copy(source, target, sems.at[i])
        for i, (source, target) in enumerate(((t_in, t_out), (s_in, s_out), (h, h_out)))
    ]
    for copy in copies:
        copy.start()
    width = CELLS // PARTS
    for i in range(PARTS):
        columns = pl.ds(i * width, width)
        for n, (source, slope, store, target) in enumerate(
            ((u_in, sx, u, u_out), (v_in, sy, v, v_out))
        ):
            for level in range(LEVELS):
                rows = pl.ds(level * SLOTS, SLOTS)
                store[rows, columns] = source[rows, columns] - slope[:, columns]
            copy = pltpu.make_async_copy(
                store.at[:, columns], target.at[:, columns], sems.at[3 + 2 * i + n]
            )
            copy.start()
            copies.append(copy)
    for copy in copies:
        copy.wait()


def finish(fields, extras):
    vmem = pl.BlockSpec(memory_space=pltpu.VMEM)
    hbm = pl.BlockSpec(memory_space=pltpu.HBM)
    big = jax.ShapeDtypeStruct((LEVELS * SLOTS, CELLS), F32)
    small = jax.ShapeDtypeStruct((SLOTS, CELLS), F32)
    return pl.pallas_call(
        finish_kernel,
        in_specs=[vmem] * 7,
        out_specs=[hbm] * 5,
        out_shape=[big] * 4 + [small],
        scratch_shapes=[
            pltpu.VMEM((LEVELS * SLOTS, CELLS), F32),
            pltpu.VMEM((LEVELS * SLOTS, CELLS), F32),
            pltpu.SemaphoreType.DMA((3 + 2 * PARTS,)),
        ],
        compiler_params=pltpu.CompilerParams(vmem_limit_bytes=16 * 1024 * 1024),
        name="finish",
    )(*fields, *extras)


def local(sizes, t, s, u, v, k, c, g, flags, lists):
    stacked = LEVELS * SLOTS
    fields = [x.reshape(stacked, CELLS) for x in (t, s, u, v)]
    big = jax.ShapeDtypeStruct((stacked, CELLS), F32)
    small = jax.ShapeDtypeStruct((SLOTS, CELLS), F32)
    anywhere = pl.BlockSpec(memory_space=pl.ANY)
    held = pl.BlockSpec(memory_space=pltpu.HBM)
    vmem = pl.BlockSpec(memory_space=pltpu.VMEM)
    dma = pltpu.SemaphoreType.DMA
    total = sizes[0] * sizes[1]
    tall = ROWS + 2 * HALO
    results = pl.pallas_call(
        functools.partial(kernel, sizes),
        out_shape=[big] * 4 + [small] * 3,
        in_specs=[held] * 9,
        out_specs=[anywhere] * 4 + [vmem] * 3,
        scratch_shapes=[
            pltpu.VMEM((4, stacked, CELLS), F32),
            pltpu.VMEM((stacked - SLOTS, CELLS), F32),
            pltpu.VMEM((SLOTS, CELLS), F32),
            pltpu.VMEM((SLOTS, CELLS), F32),
            pltpu.VMEM((8, LANES), jnp.int32),
            pltpu.SMEM((SLOTS * total,), jnp.int32),
            pltpu.VMEM((4, stacked, CELLS), F32),
            pltpu.VMEM((stacked, CELLS), F32),
            pltpu.VMEM((stacked, CELLS), F32),
            pltpu.VMEM((stacked, CELLS), F32),
            pltpu.VMEM((4, stacked, LANES), F32),
            pltpu.VMEM((4, stacked, CELLS), F32),
            pltpu.VMEM((4, stacked, CELLS), F32),
            pltpu.VMEM((4, stacked, CELLS + 2 * LANES), F32),
            pltpu.VMEM((4, stacked, CELLS), F32),
            pltpu.VMEM((2 * LANES, 4 * LANES), BF16),
            pltpu.VMEM((2 * LANES, LANES), BF16),
            pltpu.VMEM((4, 2, stacked, LANES), F32),
            pltpu.VMEM((2, 4, 2, stacked, LANES), F32),
            pltpu.VMEM((8, SLOTS, LANES), F32),
            pltpu.VMEM((2, 8, SLOTS, LANES), F32),
            pltpu.VMEM((8, SLOTS, LANES), F32),
            pltpu.VMEM((2, 8, SLOTS, LANES), F32),
            pltpu.VMEM((PAIRS, SLOTS, LANES), F32),
            pltpu.VMEM((PAIRS, SLOTS, LANES), F32),
            pltpu.VMEM((tall, SLOTS, LANES), F32),
            pltpu.VMEM((tall, SLOTS, LANES), F32),
            pltpu.VMEM((ROWS, SLOTS, LANES), F32),
            pltpu.VMEM((tall, SLOTS, LANES), F32),
            pltpu.VMEM((tall, SLOTS, LANES), F32),
            pltpu.VMEM((tall, SLOTS, LANES), F32),
            pltpu.VMEM((tall, SLOTS, LANES), F32),
            pltpu.VMEM((stacked, CELLS), F32),
            pltpu.VMEM((PAIRS, 16, 2 * LANES), BF16),
            pltpu.VMEM((4, SLOTS, LANES), F32),
            pltpu.VMEM((2, 8, LANES), F32),
            pltpu.VMEM((2, 16, LANES), F32),
            dma((9,)),
            dma((4,)),
            dma((2, 4)),
            dma((2, 4)),
            dma((2,)),
            dma((2,)),
            dma((2,)),
            dma((2,)),
            dma((4,)),
            dma((4,)),
        ],
        compiler_params=pltpu.CompilerParams(
            collective_id=0, has_side_effects=True, vmem_limit_bytes=40 * 1024 * 1024
        ),
        name="ocean_step",
    )(
        *[
            pltpu.with_memory_space_constraint(x, pltpu.HBM)
            for x in (*fields, k.reshape(stacked - SLOTS, CELLS), c, g, flags, lists.T)
        ],
    )
    done = finish(results[:4], results[4:])
    shape = (LEVELS, SLOTS, CELLS)
    return tuple(x.reshape(shape) for x in done[:4]) + (done[4],)


def solution(mesh):
    whole = P(None, ("gx", "gy"), None)
    flat = P(("gx", "gy"), None)
    return jax.shard_map(
        functools.partial(local, (mesh.shape["gx"], mesh.shape["gy"])),
        mesh=mesh,
        in_specs=(whole, whole, whole, whole, whole, flat, flat, P(), P()),
        out_specs=(whole, whole, whole, whole, flat),
        check_vma=False,
    )
```

```python
import functools
import itertools

import jax
import jax.numpy as jnp
from jax import lax
from jax.experimental import pallas as pl
from jax.experimental.pallas import tpu as pltpu
from jax.sharding import PartitionSpec as P

MESH = pl.DeviceIdType.MESH
F32 = jnp.float32
BF16 = jnp.bfloat16
LANES = 128
SLOTS = 8
LEVELS = 8
PAIRS = 32
CELLS = 4096
ROWS = 64
HALO = 4
CHUNK = 8
PARTS = 4


def tile(t):
    return pl.ds(pl.multiple_of(t * LANES, LANES), LANES)


def kernel(
    sizes,
    t_in, s_in, u_in, v_in, k_in, c_in, g_in, flags_in, lists,
    t_out, s_out, u_out, v_out, sx_out, sy_out, h_out,
    q, kk, cc, src, own_lists, flags, mixed, ip, fu, gl, hx,
    east_of, west_of, half_of, edge_of, shifts, spread,
    strips, arrived, mstrips, marrived, zstrips, zarrived,
    z2, mi2, zx, mx, mrow, v1, v2, v3, v4, inward, choose, part, near_sums, far_sums,
    in_sem, out_sem, strip_send, strip_recv, m_send, m_recv, z_send, z_recv, sum_send, sum_recv,
):
    count_x, count_y = sizes
    total = count_x * count_y
    gx, gy = lax.axis_index("gx"), lax.axis_index("gy")
    pos = gx * count_y + gy
    before, after = (pos + total - 1) % total, (pos + 1) % total
    ring = [(before // count_y, before % count_y), (after // count_y, after % count_y)]

    ys = [(gx + n) % 4 for n in range(4)]
    zs = [(gy // 8 + n) % 4 * 8 for n in range(4)]
    xs = [(gy // 2 + n) % 4 * 2 for n in range(4)]
    cores = [(gy + n) % 2 for n in range(2)]

    def hops(step):
        return -sum(min(n, 4 - n) for n in step)

    near_steps = sorted(itertools.product((0, 2, 1, 3), range(2)), key=lambda step: hops(step[:1]))
    far_steps = sorted(itertools.product(range(4), range(4)), key=hops)
    near = [(gx, zs[0] + xs[x] + cores[c]) for x, c in near_steps if x or c]
    far = [(ys[y], zs[z] + xs[0] + cores[0]) for y, z in far_steps if y or z]
    groups = ((near, gy % 8), (far, gx * 4 + gy // 8))
    partners = ring + far + near

    barrier = pltpu.get_barrier_semaphore()

    loads = []
    for number, ref in enumerate((t_in, s_in, u_in, v_in)):
        loads.append(pltpu.make_async_copy(ref, q.at[number], in_sem.at[number]))
    loads.append(pltpu.make_async_copy(
            lists.at[:, tile(pos // (LANES // SLOTS))], own_lists, in_sem.at[4]
        ))
    loads.append(pltpu.make_async_copy(c_in, cc, in_sem.at[5]))
    loads.append(pltpu.make_async_copy(k_in, kk, in_sem.at[6]))
    loads.append(pltpu.make_async_copy(g_in, src, in_sem.at[7]))
    for load in loads[:2]:
        load.start()
    for other in partners:
        pl.semaphore_signal(barrier, inc=1, device_id=other, device_id_type=MESH)
    for load in loads[2:]:
        load.start()
    flag_load = pltpu.make_async_copy(flags_in, flags, in_sem.at[8])
    flag_load.start()

    lane = lax.broadcasted_iota(jnp.int32, (SLOTS, LANES), 1)
    slot = lax.broadcasted_iota(jnp.int32, (SLOTS, LANES), 0)
    low_half = lane < ROWS
    lane_all = lax.broadcasted_iota(jnp.int32, (LEVELS * SLOTS, LANES), 1)

    def send_strips(number):
        copies = []
        for side in range(2):
            copy = pltpu.make_async_remote_copy(
                src_ref=strips.at[number],
                dst_ref=arrived.at[1 - side, number],
                send_sem=strip_send.at[side, number],
                recv_sem=strip_recv.at[1 - side, number],
                device_id=ring[side],
                device_id_type=MESH,
            )
            copy.start()
            copies.append(copy)
        return copies

    row = lax.broadcasted_iota(jnp.int32, (2 * LANES, LANES), 0) % LANES
    column = lax.broadcasted_iota(jnp.int32, (2 * LANES, LANES), 1)
    odd = column % 2 == 1
    upper_odd = (column >= 63) & (column < 127)
    packing = jnp.where(
        odd, jnp.where(upper_odd, 63, 127), jnp.where(column < ROWS, 0, ROWS)
    )
    edge_row = row % 2 == 1
    target = jnp.where(
        edge_row,
        jnp.where((row >= 63) & (row < 127), 0, ROWS),
        jnp.where(row < ROWS, 63, 127),
    )
    for place, chosen_lanes in enumerate(
        (
            (row == column + 1) & (column % ROWS != ROWS - 1),
            (row == column - 1) & (column % ROWS != 0),
            row == (column + ROWS) % LANES,
            row == packing,
        )
    ):
        shifts[:, place * LANES : (place + 1) * LANES] = jnp.where(chosen_lanes, 1.0, 0.0).astype(BF16)
    spread[...] = jnp.where(column == target, 1.0, 0.0).astype(BF16)

    position = lax.broadcasted_iota(jnp.int32, (16, 2 * LANES), 1)
    for t in range(PAIRS):
        choose[t] = jnp.where((((position + 1) & 63) >> 1) == t, 1.0, 0.0).astype(BF16)

    def parts(value):
        high = value.astype(BF16)
        rest = (value - high.astype(F32)).astype(BF16)
        return jnp.concatenate([high, rest], axis=1)

    stacked = LEVELS * SLOTS
    strip_copies = [None] * 4

    def shift_field(number):
        def shift_all(chunk, acc):
            first = chunk * CHUNK
            pieces = []
            for i in range(CHUNK):
                value = q[number, :, tile(first + i)]
                if number == 0:
                    value = value - q[1, :, tile(first + i)]
                    q[0, :, tile(first + i)] = value
                pieces.append(parts(value))
            split_parts = jnp.concatenate(pieces, axis=0)
            moved = jnp.dot(split_parts, shifts[...], preferred_element_type=F32)
            for i in range(CHUNK):
                rows = slice(i * stacked, (i + 1) * stacked)
                east_of[number, :, tile(first + i)] = moved[rows, :LANES]
                west_of[number, :, tile(first + i)] = moved[rows, LANES : 2 * LANES]
                half_of[number, :, tile(first + i + 1)] = moved[rows, 2 * LANES : 3 * LANES]
                here = (((lane_all + 1) & 63) >> 1) == first + i
                acc = jnp.where(here, moved[rows, 3 * LANES :], acc)
            return acc

        strips[number, 0] = lax.fori_loop(
            0, PAIRS // CHUNK, shift_all, jnp.zeros((stacked, LANES), F32), unroll=4
        )
        for t in (0, PAIRS + 1):
            half_of[number, :, tile(t)] = jnp.zeros((stacked, LANES), F32)
        strips[number, 1] = jnp.where(
            lane_all < ROWS, q[number, :, tile(0)], q[number, :, tile(PAIRS - 1)]
        )

    loads[0].wait()
    loads[1].wait()
    shift_field(0)
    pl.semaphore_wait(barrier, len(partners))
    strip_copies[0] = send_strips(0)

    flag_load.wait()
    weight = jnp.zeros((SLOTS, LANES), F32)
    for b in range(SLOTS):
        flag = jnp.where(flags[pos * SLOTS + b] > 0, 1.0, 0.0)
        weight = jnp.where(slot == b, flag, weight)

    loads[4].wait()
    loads[5].wait()

    def wide_strips(value_of, store):
        for group in range(4):
            packed = jnp.zeros((SLOTS, LANES), F32)
            for k in range(8):
                value = value_of[8 * group + k]
                moved = pltpu.roll(value, 8 * k, 1) if k else value
                packed = jnp.where((((lane + 4) & 63) >> 3) == k, moved, packed)
            store[group] = packed
        for place, t in enumerate((0, 1, PAIRS - 2, PAIRS - 1)):
            store[4 + place] = value_of[t]

    def diagonal(t, _):
        centre = 6.0 + cc[:, tile(t)]
        mi2[t] = weight / centre
        mrow[2 * t] = jnp.where(low_half, centre, 0.0)
        mrow[2 * t + 1] = jnp.where(low_half, pltpu.roll(centre, 64, 1), 0.0)
        return 0

    lax.fori_loop(0, PAIRS, diagonal, 0, unroll=8)
    wide_strips(mi2, mstrips)

    def exchange(store, landing, send_sem, recv_sem):
        copies = []
        for side in range(2):
            copy = pltpu.make_async_remote_copy(
                src_ref=store,
                dst_ref=landing.at[1 - side],
                send_sem=send_sem.at[side],
                recv_sem=recv_sem.at[1 - side],
                device_id=ring[side],
                device_id_type=MESH,
            )
            copy.start()
            copies.append(copy)
        return copies

    m_copies = exchange(mstrips, marrived, m_send, m_recv)

    listed_lanes = pltpu.roll(
        own_lists[...].astype(F32), (LANES - (pos % (LANES // SLOTS)) * SLOTS) % LANES, 1
    )
    chosen = []
    for direction in range(8):
        line = jnp.broadcast_to(listed_lanes[direction : direction + 1], (SLOTS, LANES))
        own = jnp.sum(jnp.where(lane == slot, line, 0.0), axis=1, keepdims=True)
        listed = jnp.broadcast_to(own, (SLOTS, LANES)).astype(jnp.int32)
        column = (listed - (pos - 1) * SLOTS + total * SLOTS) % (total * SLOTS)
        there = listed >= 0
        which = column // SLOTS
        row = jnp.where(there, column % SLOTS, 0)
        chosen.append((row, [there & (which == side) for side in range(3)]))

    def take(direction, sources):
        row, sides = chosen[direction]
        result = jnp.zeros((SLOTS, LANES), F32)
        for source, side in zip(sources, sides):
            result = jnp.where(side, jnp.take_along_axis(source, row, axis=0), result)
        return result

    east_edge = (lane & 63) == 63
    west_edge = (lane & 63) == 0

    def inside(numbers, t):
        total_gap = jnp.zeros((SLOTS, LANES), F32)
        for level in range(LEVELS):
            rows = pl.ds(level * SLOTS, SLOTS)
            zonal = q[2, rows, tile(t)]
            meridional = q[3, rows, tile(t)]
            from_west = zonal > 0.0
            from_south = meridional > 0.0
            behind = low_half & from_south
            beyond = jnp.logical_not(low_half | from_south)
            speed_x = jnp.abs(zonal)
            speed_y = jnp.abs(meridional)
            stay = 1.0 - speed_x - speed_y
            if 0 in numbers:
                outside = (east_edge & jnp.logical_not(from_west)) | (west_edge & from_west)
                inward[rows, tile(t)] = jnp.where(outside, speed_x, 0.0)
            for number in numbers:
                along = jnp.where(from_west, west_of[number, rows, tile(t)], east_of[number, rows, tile(t)])
                across = jnp.where(beyond, half_of[number, rows, tile(t + 2)], half_of[number, rows, tile(t + 1)])
                across = jnp.where(behind, half_of[number, rows, tile(t)], across)
                moved = stay * q[number, rows, tile(t)] + speed_x * along + speed_y * across
                east_of[number, rows, tile(t)] = moved
                if number == 0:
                    total_gap = total_gap + moved
        return total_gap

    for i in (2, 3, 7):
        loads[i].wait()

    def first_load(t, _):
        z2[t] = src[:, tile(t)] + inside((0,), t) * (1.0 / LEVELS)
        return 0

    lax.fori_loop(0, PAIRS, first_load, 0)

    def share(use, group, value):
        phase = 2 * use + group
        peers, own = groups[group]
        store, landing = part.at[phase], (near_sums, far_sums)[group].at[use]
        store[0:1] = value
        landing[pl.ds(own, 1)] = value
        for peer in peers:
            pltpu.make_async_remote_copy(
                src_ref=store.at[pl.ds(0, 1)],
                dst_ref=landing.at[pl.ds(own, 1)],
                send_sem=sum_send.at[phase],
                recv_sem=sum_recv.at[phase],
                device_id=peer,
                device_id_type=MESH,
            ).start()

    def gather_sum(use, group):
        phase = 2 * use + group
        peers, _ = groups[group]
        landing = (near_sums, far_sums)[group].at[use]
        every = landing.at[pl.ds(0, len(peers))]
        copies = pltpu.make_async_remote_copy(
            src_ref=every,
            dst_ref=every,
            send_sem=sum_send.at[phase],
            recv_sem=sum_recv.at[phase],
            device_id=ring[0],
            device_id_type=MESH,
        )
        copies.wait_recv()
        copies.wait_send()
        return jnp.sum(landing[...], axis=0, keepdims=True)

    def spread_out(sums):
        return [jnp.broadcast_to(sums[:, i : i + 1], (SLOTS, LANES)) for i in range(8)]

    def gathered(values):
        result = jnp.zeros((SLOTS, LANES), F32)
        for place, value in enumerate(values):
            result = jnp.where(slot == place, jnp.sum(value, axis=0, keepdims=True), result)
        column = jnp.sum(result, axis=1, keepdims=True)
        return jnp.sum(jnp.where(lane == slot, column, 0.0), axis=0, keepdims=True)

    zero = jnp.zeros((SLOTS, LANES), F32)

    def split(t, carry):
        last, line, norm, product = carry
        value = z2[t] * mi2[t]
        for row, moved in ((2 * t, value), (2 * t + 1, pltpu.roll(value, 64, 1))):
            here = jnp.where(low_half, moved, 0.0)
            ahead = pltpu.roll(here, LANES - 1, 1)
            wide = here + 0.5 * (ahead + pltpu.roll(here, 1, 1))
            norm = norm + here * here * mrow[row]
            product = product + (here * ahead + last * wide)
            last = here
        return last, line, norm, product

    _, _, norm, product = lax.fori_loop(0, PAIRS, split, (zero, zero, zero, zero), unroll=8)
    share(0, 0, gathered([norm, 2.0 * product]))

    for number in (1, 2, 3):
        shift_field(number)

    def fill_halos(number):
        for copy in strip_copies[number]:
            copy.wait()

        for level in range(LEVELS):
            rows = pl.ds(level * SLOTS, SLOTS)
            sides = [arrived[0, number, 0, rows], strips[number, 0, rows], arrived[1, number, 0, rows]]
            hx[number, rows] = jnp.where((lane & 1) == 1, take(1, sides), take(0, sides))
            ends = [arrived[0, number, 1, rows], strips[number, 1, rows], arrived[1, number, 1, rows]]
            end = jnp.where(low_half, take(2, ends), take(3, ends))
            end = pltpu.roll(end, 64, 1)
            first = q[3, rows, tile(0)]
            last = q[3, rows, tile(PAIRS - 1)]
            below = jnp.where(low_half & (first > 0.0), first, 0.0) * end
            above = jnp.where(low_half | (last > 0.0), 0.0, -last) * end
            east_of[number, rows, tile(0)] += below
            east_of[number, rows, tile(PAIRS - 1)] += above
            if number == 0:
                z2[0] += below * (1.0 / LEVELS)
                z2[PAIRS - 1] += above * (1.0 / LEVELS)
        halo_parts = parts(hx[number])

        for chunk in range(PAIRS // CHUNK):
            first = chunk * CHUNK
            pieces = []
            for i in range(CHUNK):
                pieces += [halo_parts[16 * j : 16 * j + 16] * choose[first + i] for j in range(4)]
            found = jnp.dot(
                jnp.concatenate(pieces, axis=0), spread[...], preferred_element_type=F32
            )
            for i in range(CHUNK):
                edge_of[number, :, tile(first + i)] = found[i * stacked : (i + 1) * stacked]

    def advance(numbers, t):
        carried = {number: [] for number in numbers}
        for level in range(LEVELS):
            rows = pl.ds(level * SLOTS, SLOTS)
            inverse = ip[rows, tile(t)]
            entering = inward[rows, tile(t)]
            for number in numbers:
                moved = east_of[number, rows, tile(t)] + entering * edge_of[number, rows, tile(t)]
                value = moved * inverse
                if level > 0:
                    value = value + gl[rows, tile(t)] * carried[number][-1]
                carried[number].append(value)
        solved = {}
        for number in numbers:
            values = carried[number]
            for level in range(LEVELS - 2, -1, -1):
                rows = pl.ds(level * SLOTS, SLOTS)
                values[level] = values[level] + fu[rows, tile(t)] * values[level + 1]
            solved[number] = values
        for number in numbers:
            for level in range(LEVELS):
                value = solved[number][level]
                if number == 0:
                    value = value + solved[1][level]
                mixed[number, pl.ds(level * SLOTS, SLOTS), tile(t)] = value

    outs = (t_out, s_out, u_out, v_out)

    def write_out(number):
        copy = pltpu.make_async_copy(mixed.at[number], outs[number], out_sem.at[number])
        copy.start()
        return copy

    fill_halos(0)

    def whole_load(t, _):
        entering = jnp.zeros((SLOTS, LANES), F32)
        for level in range(LEVELS):
            rows = pl.ds(level * SLOTS, SLOTS)
            entering = entering + inward[rows, tile(t)] * edge_of[0, rows, tile(t)]
        z2[t] = (z2[t] + entering * (1.0 / LEVELS)) * mi2[t]
        return 0

    lax.fori_loop(0, PAIRS, whole_load, 0, unroll=16)
    wide_strips(z2, zstrips)
    z_copies = exchange(zstrips, zarrived, z_send, z_recv)
    for number in (1, 2, 3):
        strip_copies[number] = send_strips(number)
    share(0, 1, gather_sum(0, 0))

    def others_inside(t, _):
        inside((1, 2, 3), t)
        return 0

    lax.fori_loop(0, PAIRS, others_inside, 0)


    def widen(store, landing, halves, wide, interior):
        def sources(place):
            return [landing[0, place], store[place], landing[1, place]]

        for first, directions, places in (
            (0, (3, 6, 7), (6, 7)),
            (HALO + ROWS, (2, 4, 5), (4, 5)),
        ):
            for i, place in enumerate(places):
                line = take(directions[0], sources(place))
                corner = jnp.where(
                    (lane & 63) < 32,
                    take(directions[1], sources(place)),
                    take(directions[2], sources(place)),
                )
                wide[first + 2 * i] = jnp.where(low_half, line, pltpu.roll(corner, 64, 1))
                wide[first + 2 * i + 1] = jnp.where(low_half, pltpu.roll(line, 64, 1), corner)
        for group in range(4):
            halves[group] = jnp.where(
                (lane & 4) == 0, take(0, sources(group)), take(1, sources(group))
            )

        def rows(t, _):
            side = halves[t // 8]
            step = (8 * t) % ROWS
            even, odd = interior(t)
            wide[HALO + 2 * t] = jnp.where(low_half, even, pltpu.roll(side, 64 - step, 1))
            wide[HALO + 2 * t + 1] = jnp.where(
                low_half, odd, pltpu.roll(side, (LANES - step) % LANES, 1)
            )
            return 0

        lax.fori_loop(0, PAIRS, rows, 0, unroll=32)

    for copy in m_copies:
        copy.wait()
    widen(mstrips, marrived, v1, mx, lambda t: (mi2[t], pltpu.roll(mi2[t], 64, 1)))
    for copy in z_copies:
        copy.wait()
    widen(
        zstrips, zarrived, v1, zx,
        lambda t: (z2[t], pltpu.roll(z2[t], 64, 1)),
    )

    def neighbours(value):
        paired = pltpu.roll(value, 1, 1) + pltpu.roll(value, LANES - 1, 1)
        return paired, value + 0.5 * paired

    basis = [zx, v1, v2, v3, v4]
    moments = []
    shift = None
    for power in range(4):
        old, new = basis[power], basis[power + 1]
        first, last = 1 + power, HALO + ROWS + 2 - power
        def read(a, power=power, old=old, shift=shift):
            value = old[a]
            if power:
                value = value - shift * basis[power - 1][a]
                old[a] = value
            return value

        def advance_row(a, carry, new=new, read=read):
            here, paired, wide, behind = carry
            ahead = read(a + 1)
            ahead_paired, ahead_wide = neighbours(ahead)
            value = mx[a] * (paired + behind + ahead_wide)
            new[a] = value
            return (ahead, ahead_paired, ahead_wide, wide), here, value

        behind = read(first - 1)
        here = read(first)
        carry = (here, *neighbours(here), neighbours(behind)[1])
        for a in range(first, HALO):
            carry, _, _ = advance_row(a, carry)

        def inner(r, state, power=power, advance_row=advance_row, shift=shift):
            carry, same, cross = state
            carry, here, value = advance_row(r + HALO, carry)
            weighed = mrow[r] * here
            if power == 0:
                return carry, same + here * weighed, cross
            if power == 3:
                value = value - shift * here
                return carry, same + here * weighed, (cross[0] + basis[2][r + HALO] * weighed, cross[1] + weighed * value)
            return carry, same + here * weighed, cross + basis[power - 1][r + HALO] * weighed

        start = (zero, zero) if power == 3 else zero
        carry, same, cross = lax.fori_loop(0, ROWS, inner, (carry, zero, start), unroll=64)
        if power:
            moments.append(cross[0] if power == 3 else cross)
        moments.append(same)
        if power == 3:
            moments.append(cross[1])
        for a in range(HALO + ROWS, last + 1):
            carry, _, _ = advance_row(a, carry)
        if power == 0:
            both = spread_out(gather_sum(0, 1))
            shift = both[1] / both[0]

    share(1, 0, gathered(moments))
    fill_halos(1)

    loads[6].wait()

    def factor(t, _):
        above = None
        for level in range(LEVELS):
            rows = pl.ds(level * SLOTS, SLOTS)
            pivot = 1.0
            if level > 0:
                lower = kk[pl.ds((level - 1) * SLOTS, SLOTS), tile(t)]
                pivot = pivot + lower
            if level < LEVELS - 1:
                upper = kk[rows, tile(t)]
                pivot = pivot + upper
            if level > 0:
                pivot = pivot - lower * above
            inverse = 1.0 / pivot
            ip[rows, tile(t)] = inverse * weight
            if level > 0:
                gl[rows, tile(t)] = lower * inverse
            if level < LEVELS - 1:
                above = upper * inverse
                fu[rows, tile(t)] = above
        return 0

    lax.fori_loop(0, PAIRS, factor, 0, unroll=2)

    def tracers(t, _):
        advance((0, 1), t)
        return 0

    lax.fori_loop(0, PAIRS, tracers, 0)
    out_copies = [write_out(0), write_out(1)]
    share(1, 1, gather_sum(1, 0))

    fill_halos(2)
    fill_halos(3)

    def velocities(t, _):
        advance((2, 3), t)
        return 0

    lax.fori_loop(0, PAIRS, velocities, 0)
    out_copies += [write_out(2), write_out(3)]
    mu = spread_out(gather_sum(1, 1))

    rest = 1.0 - shift
    matrix = [[rest * mu[i + j] - mu[i + j + 1] for j in range(4)] for i in range(4)]
    lower = [[None] * 4 for _ in range(4)]
    pivots, inverses, ahead = [], [], []
    for j in range(4):
        pivot = matrix[j][j]
        for i in range(j):
            pivot = pivot - lower[j][i] * lower[j][i] * pivots[i]
        kept = pivot > 1e-6 * matrix[j][j]
        pivots.append(jnp.where(kept, pivot, 0.0) if j else pivot)
        inverses.append(jnp.where(kept, 1.0 / pivot, 0.0) if j else 1.0 / pivot)
        for i in range(j + 1, 4):
            entry = matrix[i][j]
            for m in range(j):
                entry = entry - lower[i][m] * lower[j][m] * pivots[m]
            lower[i][j] = entry * inverses[j]
        right = mu[j]
        for i in range(j):
            right = right - lower[j][i] * ahead[i]
        ahead.append(right)
    factors = [None] * 4
    for j in range(3, -1, -1):
        value = ahead[j] * inverses[j]
        for i in range(j + 1, 4):
            value = value - lower[i][j] * factors[i]
        factors[j] = value

    def level_row(a):
        value = factors[0] * basis[0][a]
        for j in range(1, 4):
            value = value + factors[j] * basis[j][a]
        return value

    def slopes(t, carry):
        behind, here = carry
        ahead = level_row(HALO + 2 * t + 1)
        beyond = level_row(HALO + 2 * t + 2)

        def zonal_slope(value):
            return 0.5 * (pltpu.roll(value, LANES - 1, 1) - pltpu.roll(value, 1, 1))

        def joined(even, odd):
            return jnp.where(low_half, even, pltpu.roll(odd, 64, 1))

        sx_out[:, tile(t)] = joined(zonal_slope(here), zonal_slope(ahead))
        sy_out[:, tile(t)] = joined(0.5 * (ahead - behind), 0.5 * (beyond - here))
        h_out[:, tile(t)] = joined(here, ahead)
        return ahead, beyond

    lax.fori_loop(0, PAIRS, slopes, (level_row(HALO - 1), level_row(HALO)), unroll=32)
    for copy in out_copies:
        copy.wait()


def finish_kernel(t_in, s_in, u_in, v_in, sx, sy, h, t_out, s_out, u_out, v_out, h_out, u, v, sems):
    copies = [
        pltpu.make_async_copy(source, target, sems.at[i])
        for i, (source, target) in enumerate(((t_in, t_out), (s_in, s_out), (h, h_out)))
    ]
    for copy in copies:
        copy.start()
    width = CELLS // PARTS
    for i in range(PARTS):
        columns = pl.ds(i * width, width)
        for n, (source, slope, store, target) in enumerate(
            ((u_in, sx, u, u_out), (v_in, sy, v, v_out))
        ):
            for level in range(LEVELS):
                rows = pl.ds(level * SLOTS, SLOTS)
                store[rows, columns] = source[rows, columns] - slope[:, columns]
            copy = pltpu.make_async_copy(
                store.at[:, columns], target.at[:, columns], sems.at[3 + 2 * i + n]
            )
            copy.start()
            copies.append(copy)
    for copy in copies:
        copy.wait()


def finish(fields, extras):
    vmem = pl.BlockSpec(memory_space=pltpu.VMEM)
    hbm = pl.BlockSpec(memory_space=pltpu.HBM)
    big = jax.ShapeDtypeStruct((LEVELS * SLOTS, CELLS), F32)
    small = jax.ShapeDtypeStruct((SLOTS, CELLS), F32)
    return pl.pallas_call(
        finish_kernel,
        in_specs=[vmem] * 7,
        out_specs=[hbm] * 5,
        out_shape=[big] * 4 + [small],
        scratch_shapes=[
            pltpu.VMEM((LEVELS * SLOTS, CELLS), F32),
            pltpu.VMEM((LEVELS * SLOTS, CELLS), F32),
            pltpu.SemaphoreType.DMA((3 + 2 * PARTS,)),
        ],
        compiler_params=pltpu.CompilerParams(vmem_limit_bytes=16 * 1024 * 1024),
        name="finish",
    )(*fields, *extras)


def local(sizes, t, s, u, v, k, c, g, flags, lists):
    stacked = LEVELS * SLOTS
    fields = [x.reshape(stacked, CELLS) for x in (t, s, u, v)]
    big = jax.ShapeDtypeStruct((stacked, CELLS), F32)
    small = jax.ShapeDtypeStruct((SLOTS, CELLS), F32)
    anywhere = pl.BlockSpec(memory_space=pl.ANY)
    held = pl.BlockSpec(memory_space=pltpu.HBM)
    vmem = pl.BlockSpec(memory_space=pltpu.VMEM)
    dma = pltpu.SemaphoreType.DMA
    total = sizes[0] * sizes[1]
    tall = ROWS + 2 * HALO
    results = pl.pallas_call(
        functools.partial(kernel, sizes),
        out_shape=[big] * 4 + [small] * 3,
        in_specs=[held] * 9,
        out_specs=[anywhere] * 4 + [vmem] * 3,
        scratch_shapes=[
            pltpu.VMEM((4, stacked, CELLS), F32),
            pltpu.VMEM((stacked - SLOTS, CELLS), F32),
            pltpu.VMEM((SLOTS, CELLS), F32),
            pltpu.VMEM((SLOTS, CELLS), F32),
            pltpu.VMEM((8, LANES), jnp.int32),
            pltpu.SMEM((SLOTS * total,), jnp.int32),
            pltpu.VMEM((4, stacked, CELLS), F32),
            pltpu.VMEM((stacked, CELLS), F32),
            pltpu.VMEM((stacked, CELLS), F32),
            pltpu.VMEM((stacked, CELLS), F32),
            pltpu.VMEM((4, stacked, LANES), F32),
            pltpu.VMEM((4, stacked, CELLS), F32),
            pltpu.VMEM((4, stacked, CELLS), F32),
            pltpu.VMEM((4, stacked, CELLS + 2 * LANES), F32),
            pltpu.VMEM((4, stacked, CELLS), F32),
            pltpu.VMEM((2 * LANES, 4 * LANES), BF16),
            pltpu.VMEM((2 * LANES, LANES), BF16),
            pltpu.VMEM((4, 2, stacked, LANES), F32),
            pltpu.VMEM((2, 4, 2, stacked, LANES), F32),
            pltpu.VMEM((8, SLOTS, LANES), F32),
            pltpu.VMEM((2, 8, SLOTS, LANES), F32),
            pltpu.VMEM((8, SLOTS, LANES), F32),
            pltpu.VMEM((2, 8, SLOTS, LANES), F32),
            pltpu.VMEM((PAIRS, SLOTS, LANES), F32),
            pltpu.VMEM((PAIRS, SLOTS, LANES), F32),
            pltpu.VMEM((tall, SLOTS, LANES), F32),
            pltpu.VMEM((tall, SLOTS, LANES), F32),
            pltpu.VMEM((ROWS, SLOTS, LANES), F32),
            pltpu.VMEM((tall, SLOTS, LANES), F32),
            pltpu.VMEM((tall, SLOTS, LANES), F32),
            pltpu.VMEM((tall, SLOTS, LANES), F32),
            pltpu.VMEM((tall, SLOTS, LANES), F32),
            pltpu.VMEM((stacked, CELLS), F32),
            pltpu.VMEM((PAIRS, 16, 2 * LANES), BF16),
            pltpu.VMEM((4, SLOTS, LANES), F32),
            pltpu.VMEM((2, 8, LANES), F32),
            pltpu.VMEM((2, 16, LANES), F32),
            dma((9,)),
            dma((4,)),
            dma((2, 4)),
            dma((2, 4)),
            dma((2,)),
            dma((2,)),
            dma((2,)),
            dma((2,)),
            dma((4,)),
            dma((4,)),
        ],
        compiler_params=pltpu.CompilerParams(
            collective_id=0, has_side_effects=True, vmem_limit_bytes=40 * 1024 * 1024
        ),
        name="ocean_step",
    )(
        *[
            pltpu.with_memory_space_constraint(x, pltpu.HBM)
            for x in (*fields, k.reshape(stacked - SLOTS, CELLS), c, g, flags, lists.T)
        ],
    )
    done = finish(results[:4], results[4:])
    shape = (LEVELS, SLOTS, CELLS)
    return tuple(x.reshape(shape) for x in done[:4]) + (done[4],)


def solution(mesh):
    whole = P(None, ("gx", "gy"), None)
    flat = P(("gx", "gy"), None)
    return jax.shard_map(
        functools.partial(local, (mesh.shape["gx"], mesh.shape["gy"])),
        mesh=mesh,
        in_specs=(whole, whole, whole, whole, whole, flat, flat, P(), P()),
        out_specs=(whole, whole, whole, whole, flat),
        check_vma=False,
    )
```

```python
import functools
import itertools

import jax
import jax.numpy as jnp
from jax import lax
from jax.experimental import pallas as pl
from jax.experimental.pallas import tpu as pltpu
from jax.sharding import PartitionSpec as P

MESH = pl.DeviceIdType.MESH
F32 = jnp.float32
BF16 = jnp.bfloat16
LANES = 128
SLOTS = 8
LEVELS = 8
PAIRS = 32
CELLS = 4096
ROWS = 64
HALO = 4
CHUNK = 8
PARTS = 4


def tile(t):
    return pl.ds(pl.multiple_of(t * LANES, LANES), LANES)


def kernel(
    sizes,
    t_in, s_in, u_in, v_in, k_in, c_in, g_in, flags_in, lists,
    t_out, s_out, u_out, v_out, sx_out, sy_out, h_out,
    q, kk, cc, src, own_lists, flags, mixed, ip, fu, gl, hx,
    east_of, west_of, half_of, edge_of, shifts, spread,
    strips, arrived, mstrips, marrived, zstrips, zarrived,
    z2, mi2, zx, mx, mrow, v1, v2, v3, v4, inward, choose, part, near_sums, far_sums,
    in_sem, out_sem, strip_send, strip_recv, m_send, m_recv, z_send, z_recv, sum_send, sum_recv,
):
    count_x, count_y = sizes
    total = count_x * count_y
    gx, gy = lax.axis_index("gx"), lax.axis_index("gy")
    pos = gx * count_y + gy
    before, after = (pos + total - 1) % total, (pos + 1) % total
    ring = [(before // count_y, before % count_y), (after // count_y, after % count_y)]

    ys = [(gx + n) % 4 for n in range(4)]
    zs = [(gy // 8 + n) % 4 * 8 for n in range(4)]
    xs = [(gy // 2 + n) % 4 * 2 for n in range(4)]
    cores = [(gy + n) % 2 for n in range(2)]

    def hops(step):
        return -sum(min(n, 4 - n) for n in step)

    near_steps = sorted(itertools.product((0, 2, 1, 3), range(2)), key=lambda step: hops(step[:1]))
    far_steps = sorted(itertools.product(range(4), range(4)), key=hops)
    near = [(gx, zs[0] + xs[x] + cores[c]) for x, c in near_steps if x or c]
    far = [(ys[y], zs[z] + xs[0] + cores[0]) for y, z in far_steps if y or z]
    groups = ((near, gy % 8), (far, gx * 4 + gy // 8))
    partners = ring + far + near

    barrier = pltpu.get_barrier_semaphore()

    loads = []
    for number, ref in enumerate((t_in, s_in, u_in, v_in)):
        loads.append(pltpu.make_async_copy(ref, q.at[number], in_sem.at[number]))
    loads.append(pltpu.make_async_copy(
            lists.at[:, tile(pos // (LANES // SLOTS))], own_lists, in_sem.at[4]
        ))
    loads.append(pltpu.make_async_copy(c_in, cc, in_sem.at[5]))
    loads.append(pltpu.make_async_copy(k_in, kk, in_sem.at[6]))
    loads.append(pltpu.make_async_copy(g_in, src, in_sem.at[7]))
    for load in loads[:2]:
        load.start()
    for other in partners:
        pl.semaphore_signal(barrier, inc=1, device_id=other, device_id_type=MESH)
    for load in loads[2:]:
        load.start()
    flag_load = pltpu.make_async_copy(flags_in, flags, in_sem.at[8])
    flag_load.start()

    lane = lax.broadcasted_iota(jnp.int32, (SLOTS, LANES), 1)
    slot = lax.broadcasted_iota(jnp.int32, (SLOTS, LANES), 0)
    low_half = lane < ROWS
    lane_all = lax.broadcasted_iota(jnp.int32, (LEVELS * SLOTS, LANES), 1)

    def send_strips(number):
        copies = []
        for side in range(2):
            copy = pltpu.make_async_remote_copy(
                src_ref=strips.at[number],
                dst_ref=arrived.at[1 - side, number],
                send_sem=strip_send.at[side, number],
                recv_sem=strip_recv.at[1 - side, number],
                device_id=ring[side],
                device_id_type=MESH,
            )
            copy.start()
            copies.append(copy)
        return copies

    row = lax.broadcasted_iota(jnp.int32, (2 * LANES, LANES), 0) % LANES
    column = lax.broadcasted_iota(jnp.int32, (2 * LANES, LANES), 1)
    odd = column % 2 == 1
    upper_odd = (column >= 63) & (column < 127)
    packing = jnp.where(
        odd, jnp.where(upper_odd, 63, 127), jnp.where(column < ROWS, 0, ROWS)
    )
    edge_row = row % 2 == 1
    target = jnp.where(
        edge_row,
        jnp.where((row >= 63) & (row < 127), 0, ROWS),
        jnp.where(row < ROWS, 63, 127),
    )
    for place, chosen_lanes in enumerate(
        (
            (row == column + 1) & (column % ROWS != ROWS - 1),
            (row == column - 1) & (column % ROWS != 0),
            row == (column + ROWS) % LANES,
            row == packing,
        )
    ):
        shifts[:, place * LANES : (place + 1) * LANES] = jnp.where(chosen_lanes, 1.0, 0.0).astype(BF16)
    spread[...] = jnp.where(column == target, 1.0, 0.0).astype(BF16)

    position = lax.broadcasted_iota(jnp.int32, (16, 2 * LANES), 1)
    for t in range(PAIRS):
        choose[t] = jnp.where((((position + 1) & 63) >> 1) == t, 1.0, 0.0).astype(BF16)

    def parts(value):
        high = value.astype(BF16)
        rest = (value - high.astype(F32)).astype(BF16)
        return jnp.concatenate([high, rest], axis=1)

    stacked = LEVELS * SLOTS
    strip_copies = [None] * 4

    def shift_field(number):
        def shift_all(chunk, acc):
            first = chunk * CHUNK
            pieces = []
            for i in range(CHUNK):
                value = q[number, :, tile(first + i)]
                if number == 0:
                    value = value - q[1, :, tile(first + i)]
                    q[0, :, tile(first + i)] = value
                pieces.append(parts(value))
            split_parts = jnp.concatenate(pieces, axis=0)
            moved = jnp.dot(split_parts, shifts[...], preferred_element_type=F32)
            for i in range(CHUNK):
                rows = slice(i * stacked, (i + 1) * stacked)
                east_of[number, :, tile(first + i)] = moved[rows, :LANES]
                west_of[number, :, tile(first + i)] = moved[rows, LANES : 2 * LANES]
                half_of[number, :, tile(first + i + 1)] = moved[rows, 2 * LANES : 3 * LANES]
                here = (((lane_all + 1) & 63) >> 1) == first + i
                acc = jnp.where(here, moved[rows, 3 * LANES :], acc)
            return acc

        strips[number, 0] = lax.fori_loop(
            0, PAIRS // CHUNK, shift_all, jnp.zeros((stacked, LANES), F32), unroll=4
        )
        for t in (0, PAIRS + 1):
            half_of[number, :, tile(t)] = jnp.zeros((stacked, LANES), F32)
        strips[number, 1] = jnp.where(
            lane_all < ROWS, q[number, :, tile(0)], q[number, :, tile(PAIRS - 1)]
        )

    loads[0].wait()
    loads[1].wait()
    shift_field(0)
    pl.semaphore_wait(barrier, len(partners))
    strip_copies[0] = send_strips(0)

    flag_load.wait()
    weight = jnp.zeros((SLOTS, LANES), F32)
    for b in range(SLOTS):
        flag = jnp.where(flags[pos * SLOTS + b] > 0, 1.0, 0.0)
        weight = jnp.where(slot == b, flag, weight)

    loads[4].wait()
    loads[5].wait()

    def wide_strips(value_of, store):
        for group in range(4):
            packed = jnp.zeros((SLOTS, LANES), F32)
            for k in range(8):
                value = value_of[8 * group + k]
                moved = pltpu.roll(value, 8 * k, 1) if k else value
                packed = jnp.where((((lane + 4) & 63) >> 3) == k, moved, packed)
            store[group] = packed
        for place, t in enumerate((0, 1, PAIRS - 2, PAIRS - 1)):
            store[4 + place] = value_of[t]

    def diagonal(t, _):
        centre = 6.0 + cc[:, tile(t)]
        mi2[t] = weight / centre
        mrow[2 * t] = jnp.where(low_half, centre, 0.0)
        mrow[2 * t + 1] = jnp.where(low_half, pltpu.roll(centre, 64, 1), 0.0)
        return 0

    lax.fori_loop(0, PAIRS, diagonal, 0, unroll=8)
    wide_strips(mi2, mstrips)

    def exchange(store, landing, send_sem, recv_sem):
        copies = []
        for side in range(2):
            copy = pltpu.make_async_remote_copy(
                src_ref=store,
                dst_ref=landing.at[1 - side],
                send_sem=send_sem.at[side],
                recv_sem=recv_sem.at[1 - side],
                device_id=ring[side],
                device_id_type=MESH,
            )
            copy.start()
            copies.append(copy)
        return copies

    m_copies = exchange(mstrips, marrived, m_send, m_recv)

    listed_lanes = pltpu.roll(
        own_lists[...].astype(F32), (LANES - (pos % (LANES // SLOTS)) * SLOTS) % LANES, 1
    )
    chosen = []
    for direction in range(8):
        line = jnp.broadcast_to(listed_lanes[direction : direction + 1], (SLOTS, LANES))
        own = jnp.sum(jnp.where(lane == slot, line, 0.0), axis=1, keepdims=True)
        listed = jnp.broadcast_to(own, (SLOTS, LANES)).astype(jnp.int32)
        column = (listed - (pos - 1) * SLOTS + total * SLOTS) % (total * SLOTS)
        there = listed >= 0
        which = column // SLOTS
        row = jnp.where(there, column % SLOTS, 0)
        chosen.append((row, [there & (which == side) for side in range(3)]))

    def take(direction, sources):
        row, sides = chosen[direction]
        result = jnp.zeros((SLOTS, LANES), F32)
        for source, side in zip(sources, sides):
            result = jnp.where(side, jnp.take_along_axis(source, row, axis=0), result)
        return result

    east_edge = (lane & 63) == 63
    west_edge = (lane & 63) == 0

    def inside(numbers, t):
        total_gap = jnp.zeros((SLOTS, LANES), F32)
        for level in range(LEVELS):
            rows = pl.ds(level * SLOTS, SLOTS)
            zonal = q[2, rows, tile(t)]
            meridional = q[3, rows, tile(t)]
            from_west = zonal > 0.0
            from_south = meridional > 0.0
            behind = low_half & from_south
            beyond = jnp.logical_not(low_half | from_south)
            speed_x = jnp.abs(zonal)
            speed_y = jnp.abs(meridional)
            stay = 1.0 - speed_x - speed_y
            if 0 in numbers:
                outside = (east_edge & jnp.logical_not(from_west)) | (west_edge & from_west)
                inward[rows, tile(t)] = jnp.where(outside, speed_x, 0.0)
            for number in numbers:
                along = jnp.where(from_west, west_of[number, rows, tile(t)], east_of[number, rows, tile(t)])
                across = jnp.where(beyond, half_of[number, rows, tile(t + 2)], half_of[number, rows, tile(t + 1)])
                across = jnp.where(behind, half_of[number, rows, tile(t)], across)
                moved = stay * q[number, rows, tile(t)] + speed_x * along + speed_y * across
                east_of[number, rows, tile(t)] = moved
                if number == 0:
                    total_gap = total_gap + moved
        return total_gap

    for i in (2, 3, 7):
        loads[i].wait()

    def first_load(t, _):
        z2[t] = src[:, tile(t)] + inside((0,), t) * (1.0 / LEVELS)
        return 0

    lax.fori_loop(0, PAIRS, first_load, 0, unroll=2)

    def share(use, group, value):
        phase = 2 * use + group
        peers, own = groups[group]
        store, landing = part.at[phase], (near_sums, far_sums)[group].at[use]
        store[0:1] = value
        landing[pl.ds(own, 1)] = value
        for peer in peers:
            pltpu.make_async_remote_copy(
                src_ref=store.at[pl.ds(0, 1)],
                dst_ref=landing.at[pl.ds(own, 1)],
                send_sem=sum_send.at[phase],
                recv_sem=sum_recv.at[phase],
                device_id=peer,
                device_id_type=MESH,
            ).start()

    def gather_sum(use, group):
        phase = 2 * use + group
        peers, _ = groups[group]
        landing = (near_sums, far_sums)[group].at[use]
        every = landing.at[pl.ds(0, len(peers))]
        copies = pltpu.make_async_remote_copy(
            src_ref=every,
            dst_ref=every,
            send_sem=sum_send.at[phase],
            recv_sem=sum_recv.at[phase],
            device_id=ring[0],
            device_id_type=MESH,
        )
        copies.wait_recv()
        copies.wait_send()
        return jnp.sum(landing[...], axis=0, keepdims=True)

    def spread_out(sums):
        return [jnp.broadcast_to(sums[:, i : i + 1], (SLOTS, LANES)) for i in range(8)]

    def gathered(values):
        result = jnp.zeros((SLOTS, LANES), F32)
        for place, value in enumerate(values):
            result = jnp.where(slot == place, jnp.sum(value, axis=0, keepdims=True), result)
        column = jnp.sum(result, axis=1, keepdims=True)
        return jnp.sum(jnp.where(lane == slot, column, 0.0), axis=0, keepdims=True)

    zero = jnp.zeros((SLOTS, LANES), F32)

    def split(t, carry):
        last, line, norm, product = carry
        value = z2[t] * mi2[t]
        for row, moved in ((2 * t, value), (2 * t + 1, pltpu.roll(value, 64, 1))):
            here = jnp.where(low_half, moved, 0.0)
            ahead = pltpu.roll(here, LANES - 1, 1)
            wide = here + 0.5 * (ahead + pltpu.roll(here, 1, 1))
            norm = norm + here * here * mrow[row]
            product = product + (here * ahead + last * wide)
            last = here
        return last, line, norm, product

    _, _, norm, product = lax.fori_loop(0, PAIRS, split, (zero, zero, zero, zero), unroll=8)
    share(0, 0, gathered([norm, 2.0 * product]))

    for number in (1, 2):
        shift_field(number)

    def fill_halos(number):
        for copy in strip_copies[number]:
            copy.wait()

        for level in range(LEVELS):
            rows = pl.ds(level * SLOTS, SLOTS)
            sides = [arrived[0, number, 0, rows], strips[number, 0, rows], arrived[1, number, 0, rows]]
            hx[number, rows] = jnp.where((lane & 1) == 1, take(1, sides), take(0, sides))
            ends = [arrived[0, number, 1, rows], strips[number, 1, rows], arrived[1, number, 1, rows]]
            end = jnp.where(low_half, take(2, ends), take(3, ends))
            end = pltpu.roll(end, 64, 1)
            first = q[3, rows, tile(0)]
            last = q[3, rows, tile(PAIRS - 1)]
            below = jnp.where(low_half & (first > 0.0), first, 0.0) * end
            above = jnp.where(low_half | (last > 0.0), 0.0, -last) * end
            east_of[number, rows, tile(0)] += below
            east_of[number, rows, tile(PAIRS - 1)] += above
            if number == 0:
                z2[0] += below * (1.0 / LEVELS)
                z2[PAIRS - 1] += above * (1.0 / LEVELS)
        halo_parts = parts(hx[number])

        for chunk in range(PAIRS // CHUNK):
            first = chunk * CHUNK
            pieces = []
            for i in range(CHUNK):
                pieces += [halo_parts[16 * j : 16 * j + 16] * choose[first + i] for j in range(4)]
            found = jnp.dot(
                jnp.concatenate(pieces, axis=0), spread[...], preferred_element_type=F32
            )
            for i in range(CHUNK):
                edge_of[number, :, tile(first + i)] = found[i * stacked : (i + 1) * stacked]

    def advance(numbers, t):
        carried = {number: [] for number in numbers}
        for level in range(LEVELS):
            rows = pl.ds(level * SLOTS, SLOTS)
            inverse = ip[rows, tile(t)]
            entering = inward[rows, tile(t)]
            for number in numbers:
                moved = east_of[number, rows, tile(t)] + entering * edge_of[number, rows, tile(t)]
                value = moved * inverse
                if level > 0:
                    value = value + gl[rows, tile(t)] * carried[number][-1]
                carried[number].append(value)
        solved = {}
        for number in numbers:
            values = carried[number]
            for level in range(LEVELS - 2, -1, -1):
                rows = pl.ds(level * SLOTS, SLOTS)
                values[level] = values[level] + fu[rows, tile(t)] * values[level + 1]
            solved[number] = values
        for number in numbers:
            for level in range(LEVELS):
                value = solved[number][level]
                if number == 0:
                    value = value + solved[1][level]
                mixed[number, pl.ds(level * SLOTS, SLOTS), tile(t)] = value

    outs = (t_out, s_out, u_out, v_out)

    def write_out(number):
        copy = pltpu.make_async_copy(mixed.at[number], outs[number], out_sem.at[number])
        copy.start()
        return copy

    fill_halos(0)

    def whole_load(t, _):
        entering = jnp.zeros((SLOTS, LANES), F32)
        for level in range(LEVELS):
            rows = pl.ds(level * SLOTS, SLOTS)
            entering = entering + inward[rows, tile(t)] * edge_of[0, rows, tile(t)]
        z2[t] = (z2[t] + entering * (1.0 / LEVELS)) * mi2[t]
        return 0

    lax.fori_loop(0, PAIRS, whole_load, 0, unroll=16)
    wide_strips(z2, zstrips)
    z_copies = exchange(zstrips, zarrived, z_send, z_recv)
    for number in (1, 2):
        strip_copies[number] = send_strips(number)
    share(0, 1, gather_sum(0, 0))
    shift_field(3)
    strip_copies[3] = send_strips(3)

    def others_inside(t, _):
        inside((1, 2, 3), t)
        return 0

    lax.fori_loop(0, PAIRS, others_inside, 0)


    def widen(store, landing, halves, wide, interior):
        def sources(place):
            return [landing[0, place], store[place], landing[1, place]]

        for first, directions, places in (
            (0, (3, 6, 7), (6, 7)),
            (HALO + ROWS, (2, 4, 5), (4, 5)),
        ):
            for i, place in enumerate(places):
                line = take(directions[0], sources(place))
                corner = jnp.where(
                    (lane & 63) < 32,
                    take(directions[1], sources(place)),
                    take(directions[2], sources(place)),
                )
                wide[first + 2 * i] = jnp.where(low_half, line, pltpu.roll(corner, 64, 1))
                wide[first + 2 * i + 1] = jnp.where(low_half, pltpu.roll(line, 64, 1), corner)
        for group in range(4):
            halves[group] = jnp.where(
                (lane & 4) == 0, take(0, sources(group)), take(1, sources(group))
            )

        def rows(t, _):
            side = halves[t // 8]
            step = (8 * t) % ROWS
            even, odd = interior(t)
            wide[HALO + 2 * t] = jnp.where(low_half, even, pltpu.roll(side, 64 - step, 1))
            wide[HALO + 2 * t + 1] = jnp.where(
                low_half, odd, pltpu.roll(side, (LANES - step) % LANES, 1)
            )
            return 0

        lax.fori_loop(0, PAIRS, rows, 0, unroll=32)

    for copy in m_copies:
        copy.wait()
    widen(mstrips, marrived, v1, mx, lambda t: (mi2[t], pltpu.roll(mi2[t], 64, 1)))
    for copy in z_copies:
        copy.wait()
    widen(
        zstrips, zarrived, v1, zx,
        lambda t: (z2[t], pltpu.roll(z2[t], 64, 1)),
    )

    def neighbours(value):
        paired = pltpu.roll(value, 1, 1) + pltpu.roll(value, LANES - 1, 1)
        return paired, value + 0.5 * paired

    basis = [zx, v1, v2, v3, v4]
    moments = []
    shift = None
    for power in range(4):
        old, new = basis[power], basis[power + 1]
        first, last = 1 + power, HALO + ROWS + 2 - power
        def read(a, power=power, old=old, shift=shift):
            value = old[a]
            if power:
                value = value - shift * basis[power - 1][a]
                old[a] = value
            return value

        def advance_row(a, carry, new=new, read=read):
            here, paired, wide, behind = carry
            ahead = read(a + 1)
            ahead_paired, ahead_wide = neighbours(ahead)
            value = mx[a] * (paired + behind + ahead_wide)
            new[a] = value
            return (ahead, ahead_paired, ahead_wide, wide), here, value

        behind = read(first - 1)
        here = read(first)
        carry = (here, *neighbours(here), neighbours(behind)[1])
        for a in range(first, HALO):
            carry, _, _ = advance_row(a, carry)

        def inner(r, state, power=power, advance_row=advance_row, shift=shift):
            carry, same, cross = state
            carry, here, value = advance_row(r + HALO, carry)
            weighed = mrow[r] * here
            if power == 0:
                return carry, same + here * weighed, cross
            if power == 3:
                value = value - shift * here
                return carry, same + here * weighed, (cross[0] + basis[2][r + HALO] * weighed, cross[1] + weighed * value)
            return carry, same + here * weighed, cross + basis[power - 1][r + HALO] * weighed

        start = (zero, zero) if power == 3 else zero
        carry, same, cross = lax.fori_loop(0, ROWS, inner, (carry, zero, start), unroll=64)
        if power:
            moments.append(cross[0] if power == 3 else cross)
        moments.append(same)
        if power == 3:
            moments.append(cross[1])
        for a in range(HALO + ROWS, last + 1):
            carry, _, _ = advance_row(a, carry)
        if power == 0:
            both = spread_out(gather_sum(0, 1))
            shift = both[1] / both[0]

    share(1, 0, gathered(moments))
    fill_halos(1)

    loads[6].wait()

    def factor(t, _):
        above = None
        for level in range(LEVELS):
            rows = pl.ds(level * SLOTS, SLOTS)
            pivot = 1.0
            if level > 0:
                lower = kk[pl.ds((level - 1) * SLOTS, SLOTS), tile(t)]
                pivot = pivot + lower
            if level < LEVELS - 1:
                upper = kk[rows, tile(t)]
                pivot = pivot + upper
            if level > 0:
                pivot = pivot - lower * above
            inverse = 1.0 / pivot
            ip[rows, tile(t)] = inverse * weight
            if level > 0:
                gl[rows, tile(t)] = lower * inverse
            if level < LEVELS - 1:
                above = upper * inverse
                fu[rows, tile(t)] = above
        return 0

    lax.fori_loop(0, PAIRS, factor, 0, unroll=2)

    def tracers(t, _):
        advance((0, 1), t)
        return 0

    lax.fori_loop(0, PAIRS, tracers, 0)
    out_copies = [write_out(0), write_out(1)]
    share(1, 1, gather_sum(1, 0))

    fill_halos(2)
    fill_halos(3)

    def velocities(t, _):
        advance((2, 3), t)
        return 0

    lax.fori_loop(0, PAIRS, velocities, 0)
    out_copies += [write_out(2), write_out(3)]
    mu = spread_out(gather_sum(1, 1))

    rest = 1.0 - shift
    matrix = [[rest * mu[i + j] - mu[i + j + 1] for j in range(4)] for i in range(4)]
    lower = [[None] * 4 for _ in range(4)]
    pivots, inverses, ahead = [], [], []
    for j in range(4):
        pivot = matrix[j][j]
        for i in range(j):
            pivot = pivot - lower[j][i] * lower[j][i] * pivots[i]
        kept = pivot > 1e-6 * matrix[j][j]
        pivots.append(jnp.where(kept, pivot, 0.0) if j else pivot)
        inverses.append(jnp.where(kept, 1.0 / pivot, 0.0) if j else 1.0 / pivot)
        for i in range(j + 1, 4):
            entry = matrix[i][j]
            for m in range(j):
                entry = entry - lower[i][m] * lower[j][m] * pivots[m]
            lower[i][j] = entry * inverses[j]
        right = mu[j]
        for i in range(j):
            right = right - lower[j][i] * ahead[i]
        ahead.append(right)
    factors = [None] * 4
    for j in range(3, -1, -1):
        value = ahead[j] * inverses[j]
        for i in range(j + 1, 4):
            value = value - lower[i][j] * factors[i]
        factors[j] = value

    def level_row(a):
        value = factors[0] * basis[0][a]
        for j in range(1, 4):
            value = value + factors[j] * basis[j][a]
        return value

    def slopes(t, carry):
        behind, here = carry
        ahead = level_row(HALO + 2 * t + 1)
        beyond = level_row(HALO + 2 * t + 2)

        def zonal_slope(value):
            return 0.5 * (pltpu.roll(value, LANES - 1, 1) - pltpu.roll(value, 1, 1))

        def joined(even, odd):
            return jnp.where(low_half, even, pltpu.roll(odd, 64, 1))

        sx_out[:, tile(t)] = joined(zonal_slope(here), zonal_slope(ahead))
        sy_out[:, tile(t)] = joined(0.5 * (ahead - behind), 0.5 * (beyond - here))
        h_out[:, tile(t)] = joined(here, ahead)
        return ahead, beyond

    lax.fori_loop(0, PAIRS, slopes, (level_row(HALO - 1), level_row(HALO)), unroll=32)
    for copy in out_copies:
        copy.wait()


def finish_kernel(t_in, s_in, u_in, v_in, sx, sy, h, t_out, s_out, u_out, v_out, h_out, u, v, sems):
    copies = [
        pltpu.make_async_copy(source, target, sems.at[i])
        for i, (source, target) in enumerate(((t_in, t_out), (s_in, s_out), (h, h_out)))
    ]
    for copy in copies:
        copy.start()
    width = CELLS // PARTS
    for i in range(PARTS):
        columns = pl.ds(i * width, width)
        for n, (source, slope, store, target) in enumerate(
            ((u_in, sx, u, u_out), (v_in, sy, v, v_out))
        ):
            for level in range(LEVELS):
                rows = pl.ds(level * SLOTS, SLOTS)
                store[rows, columns] = source[rows, columns] - slope[:, columns]
            copy = pltpu.make_async_copy(
                store.at[:, columns], target.at[:, columns], sems.at[3 + 2 * i + n]
            )
            copy.start()
            copies.append(copy)
    for copy in copies:
        copy.wait()


def finish(fields, extras):
    vmem = pl.BlockSpec(memory_space=pltpu.VMEM)
    hbm = pl.BlockSpec(memory_space=pltpu.HBM)
    big = jax.ShapeDtypeStruct((LEVELS * SLOTS, CELLS), F32)
    small = jax.ShapeDtypeStruct((SLOTS, CELLS), F32)
    return pl.pallas_call(
        finish_kernel,
        in_specs=[vmem] * 7,
        out_specs=[hbm] * 5,
        out_shape=[big] * 4 + [small],
        scratch_shapes=[
            pltpu.VMEM((LEVELS * SLOTS, CELLS), F32),
            pltpu.VMEM((LEVELS * SLOTS, CELLS), F32),
            pltpu.SemaphoreType.DMA((3 + 2 * PARTS,)),
        ],
        compiler_params=pltpu.CompilerParams(vmem_limit_bytes=16 * 1024 * 1024),
        name="finish",
    )(*fields, *extras)


def local(sizes, t, s, u, v, k, c, g, flags, lists):
    stacked = LEVELS * SLOTS
    fields = [x.reshape(stacked, CELLS) for x in (t, s, u, v)]
    big = jax.ShapeDtypeStruct((stacked, CELLS), F32)
    small = jax.ShapeDtypeStruct((SLOTS, CELLS), F32)
    anywhere = pl.BlockSpec(memory_space=pl.ANY)
    held = pl.BlockSpec(memory_space=pltpu.HBM)
    vmem = pl.BlockSpec(memory_space=pltpu.VMEM)
    dma = pltpu.SemaphoreType.DMA
    total = sizes[0] * sizes[1]
    tall = ROWS + 2 * HALO
    results = pl.pallas_call(
        functools.partial(kernel, sizes),
        out_shape=[big] * 4 + [small] * 3,
        in_specs=[held] * 9,
        out_specs=[anywhere] * 4 + [vmem] * 3,
        scratch_shapes=[
            pltpu.VMEM((4, stacked, CELLS), F32),
            pltpu.VMEM((stacked - SLOTS, CELLS), F32),
            pltpu.VMEM((SLOTS, CELLS), F32),
            pltpu.VMEM((SLOTS, CELLS), F32),
            pltpu.VMEM((8, LANES), jnp.int32),
            pltpu.SMEM((SLOTS * total,), jnp.int32),
            pltpu.VMEM((4, stacked, CELLS), F32),
            pltpu.VMEM((stacked, CELLS), F32),
            pltpu.VMEM((stacked, CELLS), F32),
            pltpu.VMEM((stacked, CELLS), F32),
            pltpu.VMEM((4, stacked, LANES), F32),
            pltpu.VMEM((4, stacked, CELLS), F32),
            pltpu.VMEM((4, stacked, CELLS), F32),
            pltpu.VMEM((4, stacked, CELLS + 2 * LANES), F32),
            pltpu.VMEM((4, stacked, CELLS), F32),
            pltpu.VMEM((2 * LANES, 4 * LANES), BF16),
            pltpu.VMEM((2 * LANES, LANES), BF16),
            pltpu.VMEM((4, 2, stacked, LANES), F32),
            pltpu.VMEM((2, 4, 2, stacked, LANES), F32),
            pltpu.VMEM((8, SLOTS, LANES), F32),
            pltpu.VMEM((2, 8, SLOTS, LANES), F32),
            pltpu.VMEM((8, SLOTS, LANES), F32),
            pltpu.VMEM((2, 8, SLOTS, LANES), F32),
            pltpu.VMEM((PAIRS, SLOTS, LANES), F32),
            pltpu.VMEM((PAIRS, SLOTS, LANES), F32),
            pltpu.VMEM((tall, SLOTS, LANES), F32),
            pltpu.VMEM((tall, SLOTS, LANES), F32),
            pltpu.VMEM((ROWS, SLOTS, LANES), F32),
            pltpu.VMEM((tall, SLOTS, LANES), F32),
            pltpu.VMEM((tall, SLOTS, LANES), F32),
            pltpu.VMEM((tall, SLOTS, LANES), F32),
            pltpu.VMEM((tall, SLOTS, LANES), F32),
            pltpu.VMEM((stacked, CELLS), F32),
            pltpu.VMEM((PAIRS, 16, 2 * LANES), BF16),
            pltpu.VMEM((4, SLOTS, LANES), F32),
            pltpu.VMEM((2, 8, LANES), F32),
            pltpu.VMEM((2, 16, LANES), F32),
            dma((9,)),
            dma((4,)),
            dma((2, 4)),
            dma((2, 4)),
            dma((2,)),
            dma((2,)),
            dma((2,)),
            dma((2,)),
            dma((4,)),
            dma((4,)),
        ],
        compiler_params=pltpu.CompilerParams(
            collective_id=0, has_side_effects=True, vmem_limit_bytes=40 * 1024 * 1024
        ),
        name="ocean_step",
    )(
        *[
            pltpu.with_memory_space_constraint(x, pltpu.HBM)
            for x in (*fields, k.reshape(stacked - SLOTS, CELLS), c, g, flags, lists.T)
        ],
    )
    done = finish(results[:4], results[4:])
    shape = (LEVELS, SLOTS, CELLS)
    return tuple(x.reshape(shape) for x in done[:4]) + (done[4],)


def solution(mesh):
    whole = P(None, ("gx", "gy"), None)
    flat = P(("gx", "gy"), None)
    return jax.shard_map(
        functools.partial(local, (mesh.shape["gx"], mesh.shape["gy"])),
        mesh=mesh,
        in_specs=(whole, whole, whole, whole, whole, flat, flat, P(), P()),
        out_specs=(whole, whole, whole, whole, flat),
        check_vma=False,
    )
```
